128 devices in a mesh: zt: 8 (over z_lo, x), xy: 16 (over z_hi, y, core).
Axes of the slice: x: 4, y: 4, z: 4 (z_hi: 2, z_lo: 2; z = z_hi * 2 + z_lo), core: 2. Of those that a mesh axis runs over, the one named last changes fastest.
Arguments:
- restricted: bfloat16 [8, 16, 64, 8, 256], P('zt', 'xy'), may hold values from -6 to 6
- stencil: bfloat16 [8, 16, 9, 64, 64, 256], P('zt', 'xy'), may hold values from -2 to 12, as said below
Outputs:
- smoothed: float32 [8, 16, 64, 8, 256], P('zt', 'xy')
The draws below stay inside these ranges and needn't reach their ends.
Inputs may be any that keep to these rules, and one draw needn't show every extreme that they name: `stencil`: entries of row i of every block at a site share a positive scale of that site and row; the self block's diagonal entries are at least 0.5.
All inputs are finite; a program needn't handle non-finite values.
Results may differ from the reference program's by a relative error of at most 0.0049.
Values may be sent and summed in bfloat16 or wider, within the bound.
No kernel may reach another device: no remote copies, remote signals or barrier semaphores. Data moves between devices by JAX's collectives and lax.ppermute only.
A program may use at most 128 MiB of HBM per device.

```python
import math
import jax
import jax.numpy as jnp

DOF = 64
NRHS = 8
LX = 16
LY = 16
SWEEPS = 4
LZ = 16
LT = 8
SITES = 256
XP = 4
BX = 4
BY = 4
BZ = 8
FINE_SITES = 256
N_ZT = 8
N_XY = 16


def draw_stencil(key, part):
    key = jax.random.fold_in(key, 11)
    scale_key, hop_key = jax.random.split(key)
    spread_factor = 0.4 / math.sqrt(9.0 * DOF)
    row_scale = jnp.exp(jax.random.uniform(scale_key, (LT, LZ, DOF, SITES), jnp.float32, 0.0, math.log(4.0)))
    hopping = jnp.clip(jax.random.normal(hop_key, (LT, LZ, 9, DOF, DOF, SITES), jnp.float32), -6.0, 6.0)
    identity_mask = (jnp.arange(DOF)[:, None] == jnp.arange(DOF)[None, :]).astype(jnp.float32)
    self_mask = (jnp.arange(9) == 0).astype(jnp.float32)
    dominant = self_mask[:, None, None, None] * identity_mask[None, :, :, None]
    full = row_scale[:, :, None, :, None, :] * (spread_factor * hopping + dominant[None, None])
    return full.astype(jnp.bfloat16)


def levels(own_key, dims, pieces, smallest, top_value):
    level = 1.0
    for position, parts in pieces:
        steps = jax.random.uniform(jax.random.fold_in(jax.random.fold_in(own_key, 6), position), (parts,), jnp.float32, smallest / len(pieces), top_value / len(pieces))
        level = level * jnp.repeat(jnp.exp(steps), dims[position] // parts).reshape((-1,) + (1,) * (len(dims) - 1 - position))
    return level


def normal_values(own_key, extent, deviation, limit, pieces=(), dtype=jnp.bfloat16):
    result = deviation * jax.random.normal(own_key, extent, jnp.float32)
    if pieces:
        result = result * levels(own_key, extent, pieces, -0.22, 0.18)
    return jnp.clip(result, -limit, limit).astype(dtype)


def setup_inputs(seed: int = 0) -> dict:
    arg_keys = jax.random.split(jax.random.key(seed), 3)
    return {
        "restricted": normal_values(arg_keys[0], (N_ZT, N_XY, DOF, NRHS, FINE_SITES), 1.0, 6.0, ((0, 8), (1, 16))),
        "stencil": draw_stencil(jax.random.fold_in(arg_keys[2], 71), 0),
    }


def apply_operator(rounded, stencil):
    planes = []
    for plane_index in range(LT):
        blocks = stencil[plane_index]
        centre = rounded[plane_index]
        neighbours = [centre,
                      jnp.roll(centre, -1, 4), jnp.roll(centre, 1, 4),
                      jnp.roll(centre, -1, 3), jnp.roll(centre, 1, 3),
                      jnp.roll(centre, -1, 0), jnp.roll(centre, 1, 0),
                      rounded[(plane_index + 1) % LT], rounded[(plane_index - 1) % LT]]
        summed = jnp.zeros((LZ, DOF, NRHS, SITES), jnp.float32)
        for term_index in range(9):
            vector_part = neighbours[term_index].reshape(LZ, DOF, NRHS, SITES).astype(jnp.float32)
            summed = summed + jnp.einsum('zoiS,zirS->zorS', blocks[:, term_index].astype(jnp.float32), vector_part)
        planes.append(summed.reshape(LZ, DOF, NRHS, LY, LX))
    return jnp.stack(planes, axis=0)


def reference(restricted, stencil):
    time_parts = LT // 2
    ordered = restricted.reshape(time_parts, 2, 4, XP, DOF, NRHS, 2, BZ, BY, BX)
    ordered = ordered.transpose(0, 6, 1, 7, 4, 5, 2, 8, 3, 9).reshape(LT, LZ, DOF, NRHS, LY, LX)
    source = ordered.astype(jnp.float32)
    diagonal = jnp.diagonal(stencil[:, :, 0], axis1=2, axis2=3)
    diagonal = jnp.moveaxis(diagonal, 3, 2).astype(jnp.float32).reshape(LT, LZ, DOF, 1, LY, LX)
    iterate = source / diagonal
    for sweep_index in range(SWEEPS - 1):
        rounded = iterate.astype(jnp.bfloat16)
        iterate = iterate + (source - apply_operator(rounded, stencil)) / diagonal
    back = iterate.reshape(time_parts, 2, 2, BZ, DOF, NRHS, 4, BY, XP, BX)
    back = back.transpose(0, 2, 6, 8, 4, 5, 1, 3, 7, 9)
    return back.reshape(LT, LZ, DOF, NRHS, FINE_SITES)
```

```python
import functools

import jax
import jax.numpy as jnp
from jax import lax
from jax.experimental import pallas as pl
from jax.experimental.pallas import tpu as pltpu
from jax.sharding import PartitionSpec as P

LX = 16
LY = 16
SWEEPS = 4
ROWS = 16
PAIR = 2
GROUP = 4
LANES = 128
F32 = jnp.float32
BF16 = jnp.bfloat16


def total(terms):
    while len(terms) > 1:
        terms = [sum(terms[i : i + 2][1:], terms[i]) for i in range(0, len(terms), 2)]
    return terms[0]


def multiply(blocks, vectors, partial_ref, write):
    _, count, _, _ = partial_ref.shape
    sixteens = 4

    @pl.loop(0, ROWS // PAIR)
    def _(pair):
        for first in range(0, count, GROUP):
            sums = {}
            for block, vector in zip(blocks, vectors):
                rows = [[block(pair * PAIR + o, i) for i in range(sixteens)] for o in range(PAIR)]
                for r in range(first, first + GROUP):
                    column = [vector(r, i) for i in range(sixteens)]
                    for o in range(PAIR):
                        term = total([a * v for a, v in zip(rows[o], column)])
                        term = (term[:8] + term[8:]).astype(F32)
                        sums[o, r] = sums[o, r] + term if (o, r) in sums else term
            for (o, r), value in sums.items():
                place = pl.ds(pl.multiple_of((pair * PAIR + o) * 8, 8), 8)
                partial_ref[0, r, place, :] = value[:, :LANES]
                partial_ref[1, r, place, :] = value[:, LANES:]

    for r in range(count):
        for half in range(2):
            parts = []
            for eight in range(ROWS // 8):
                parts.append(
                    total([partial_ref[half, r, pl.ds(eight * 64 + j, 8, stride=8), :] for j in range(8)])
                )
            write(r, half, jnp.concatenate(parts, axis=0))


def prepare_kernel(block_ref, off_ref, inverse_ref):
    rows, components, sites = block_ref.shape[1:]
    first = pl.program_id(0) * rows
    own = lax.broadcasted_iota(jnp.int32, (components, sites), 0)
    for o in range(rows):
        block = block_ref[0, o].astype(F32)
        here = own == first + o
        off_ref[o] = jnp.where(here, 0.0, block).astype(BF16)
        diagonal = jnp.sum(jnp.where(here, block, 0.0), axis=0, keepdims=True)
        inverse_ref[o : o + 1, :] = 1.0 / diagonal


def prepare(stencil):
    components, sites = stencil.shape[2:]
    return pl.pallas_call(
        prepare_kernel,
        grid=(components // ROWS,),
        in_specs=[pl.BlockSpec((1, ROWS, components, sites), lambda g: (0, g, 0, 0))],
        out_specs=[
            pl.BlockSpec((ROWS, components, sites), lambda g: (g, 0, 0)),
            pl.BlockSpec((ROWS, sites), lambda g: (g, 0)),
        ],
        out_shape=[
            jax.ShapeDtypeStruct((components, components, sites), BF16),
            jax.ShapeDtypeStruct((components, sites), F32),
        ],
        cost_estimate=pl.CostEstimate(flops=10**7, bytes_accessed=4 * 2**20, transcendentals=0),
        name="prepare",
    )(stencil)


def start_kernel(source_ref, inverse_ref, iterate_ref, rounded_ref):
    inverse = inverse_ref[...]
    for r in range(source_ref.shape[0]):
        iterate = source_ref[r].astype(F32) * inverse
        iterate_ref[r] = iterate
        rounded_ref[r] = iterate.astype(BF16)


def start(source, inverse):
    return pl.pallas_call(
        start_kernel,
        out_shape=[jax.ShapeDtypeStruct(source.shape, F32), jax.ShapeDtypeStruct(source.shape, BF16)],
        name="start",
    )(source, inverse)


def local_kernel(off_ref, hops_ref, source_ref, iterate_ref, rounded_ref, inverse_ref, base_ref, near_ref, partial_ref):
    count, components, sites = rounded_ref.shape

    @pl.when(pl.program_id(0) == 0)
    def _():
        lane = lax.broadcasted_iota(jnp.int32, (components, sites), 1) % LX
        for r in range(count):
            value = rounded_ref[r].astype(F32)
            after = jnp.where(
                lane == LX - 1, pltpu.roll(value, LX - 1, 1), pltpu.roll(value, sites - 1, 1)
            )
            before = jnp.where(lane == 0, pltpu.roll(value, sites - LX + 1, 1), pltpu.roll(value, 1, 1))
            near_ref[0, r] = after.astype(BF16)
            near_ref[1, r] = before.astype(BF16)
            near_ref[2, r] = pltpu.roll(value, sites - LX, 1).astype(BF16)
            near_ref[3, r] = pltpu.roll(value, LX, 1).astype(BF16)

    def sixteen(i):
        return slice(16 * i, 16 * i + 16)

    blocks = [lambda o, i: off_ref[o, sixteen(i), :]]
    vectors = [lambda r, i: rounded_ref[r, sixteen(i), :]]
    for k in range(4):
        blocks.append(lambda o, i, k=k: hops_ref[k, o, sixteen(i), :])
        vectors.append(lambda r, i, k=k: near_ref[k, r, sixteen(i), :])

    here = pl.ds(pl.multiple_of(pl.program_id(0) * ROWS, ROWS), ROWS)

    def write(r, half, sums):
        lanes = slice(half * LANES, half * LANES + LANES)
        left = source_ref[r, :, lanes].astype(F32) - sums
        kept = iterate_ref[r, :, lanes] - rounded_ref[r, here, lanes].astype(F32)
        base_ref[r, :, lanes] = kept + left * inverse_ref[:, lanes]

    multiply(blocks, vectors, partial_ref, write)


def local(off, stencil, source, iterate, rounded, inverse):
    count, components, sites = rounded.shape
    part = pl.BlockSpec((count, ROWS, sites), lambda g: (0, g, 0))
    return pl.pallas_call(
        local_kernel,
        grid=(components // ROWS,),
        in_specs=[
            pl.BlockSpec((ROWS, components, sites), lambda g: (g, 0, 0)),
            pl.BlockSpec((pl.Element(4), pl.Element(ROWS), pl.Element(components), pl.Element(sites)),
                         lambda g: (1, g * ROWS, 0, 0)),
            part,
            part,
            pl.BlockSpec((count, components, sites), lambda g: (0, 0, 0)),
            pl.BlockSpec((ROWS, sites), lambda g: (g, 0)),
        ],
        out_specs=part,
        out_shape=jax.ShapeDtypeStruct(rounded.shape, F32),
        scratch_shapes=[
            pltpu.VMEM((4, count, components, sites), BF16),
            pltpu.VMEM((2, count, ROWS * 8, LANES), F32),
        ],
        compiler_params=pltpu.CompilerParams(vmem_limit_bytes=40 * 2**20),
        cost_estimate=pl.CostEstimate(flops=10**9, bytes_accessed=12 * 2**20, transcendentals=0),
        name="local",
    )(off, stencil, source, iterate, rounded, inverse)


def remote_kernel(last, hops_ref, above_ref, below_ref, after_ref, earlier_ref, base_ref, inverse_ref, *rest):
    if last:
        rounded_ref, partial_ref = rest
    else:
        iterate_ref, rounded_ref, partial_ref = rest

    def sixteen(i):
        return slice(16 * i, 16 * i + 16)

    blocks, vectors = [], []
    for k, ref in enumerate((above_ref, below_ref, after_ref, earlier_ref)):
        blocks.append(lambda o, i, k=k: hops_ref[k, o, sixteen(i), :])
        vectors.append(lambda r, i, ref=ref: ref[r, sixteen(i), :])

    def write(r, half, sums):
        lanes = slice(half * LANES, half * LANES + LANES)
        iterate = base_ref[r, :, lanes] - sums * inverse_ref[:, lanes]
        if not last:
            iterate_ref[r, :, lanes] = iterate
        rounded_ref[r, :, lanes] = iterate.astype(BF16)

    multiply(blocks, vectors, partial_ref, write)


def remote(stencil, halos, base, inverse, last):
    count, components, sites = base.shape
    part = pl.BlockSpec((count, ROWS, sites), lambda g: (0, g, 0))
    whole = pl.BlockSpec((count, components, sites), lambda g: (0, 0, 0))
    types = [BF16] if last else [F32, BF16]
    return pl.pallas_call(
        functools.partial(remote_kernel, last),
        grid=(components // ROWS,),
        in_specs=[
            pl.BlockSpec((pl.Element(4), pl.Element(ROWS), pl.Element(components), pl.Element(sites)),
                         lambda g: (5, g * ROWS, 0, 0)),
            whole, whole, whole, whole,
            part,
            pl.BlockSpec((ROWS, sites), lambda g: (g, 0)),
        ],
        out_specs=[part for _ in types],
        out_shape=[jax.ShapeDtypeStruct(base.shape, t) for t in types],
        scratch_shapes=[pltpu.VMEM((2, count, ROWS * 8, LANES), F32)],
        compiler_params=pltpu.CompilerParams(vmem_limit_bytes=40 * 2**20),
        cost_estimate=pl.CostEstimate(flops=10**9, bytes_accessed=12 * 2**20, transcendentals=0),
        name="remote",
    )(stencil, *halos, base, inverse)


def neighbour(plane, axis, step):
    count = lax.axis_size(axis)
    return lax.ppermute(plane, axis, [((i + step) % count, i) for i in range(count)])


def partner(shard, axis):
    return lax.ppermute(shard, axis, [(i, i ^ 1) for i in range(lax.axis_size(axis))])


def shards(restricted, stencil):
    columns = lax.axis_size("xy")
    parts = columns // 4
    planes = columns // 2
    width = LX // parts
    height = LY // 4
    components, count = restricted.shape[2], restricted.shape[3]
    parity = lax.axis_index("zt") % 2
    stencil = stencil[0, 0]
    off, inverse = prepare(stencil)

    pieces = restricted[0, 0].reshape(components, count, 2, planes, height, width)
    kept = lax.dynamic_index_in_dim(pieces, parity, 2, keepdims=False)
    outgoing = lax.dynamic_index_in_dim(pieces, 1 - parity, 2, keepdims=False)
    incoming = partner(outgoing, "zt")
    lower = jnp.where(parity == 0, kept, incoming)
    upper = jnp.where(parity == 0, incoming, kept)
    column = jnp.concatenate([lower, upper], axis=2)[:, :, :, None]
    spread = lax.all_to_all(column, "xy", split_axis=2, concat_axis=3, tiled=True)
    spread = spread.reshape(components, count, 4, parts, height, width)
    source = spread.transpose(1, 0, 2, 4, 3, 5).reshape(count, components, LY * LX)

    iterate, rounded = start(source, inverse)
    for sweep in range(SWEEPS - 1):
        last = sweep == SWEEPS - 2
        halos = [
            neighbour(rounded, "xy", 1),
            neighbour(rounded, "xy", -1),
            neighbour(rounded, "zt", 1),
            neighbour(rounded, "zt", -1),
        ]
        base = local(off, stencil, source, iterate, rounded, inverse)
        results = remote(stencil, halos, base, inverse, last)
        if last:
            (rounded,) = results
        else:
            iterate, rounded = results

    regrouped = rounded.reshape(count, components, 4, height, parts, width)
    regrouped = regrouped.transpose(1, 0, 2, 4, 3, 5).reshape(components, count, 1, columns, height, width)
    returned = lax.all_to_all(regrouped, "xy", split_axis=3, concat_axis=2, tiled=True)[:, :, :, 0]
    own = lax.dynamic_slice_in_dim(returned, parity * planes, planes, 2)
    other = lax.dynamic_slice_in_dim(returned, (1 - parity) * planes, planes, 2)
    other = partner(other, "zt")
    first = jnp.where(parity == 0, own, other)
    second = jnp.where(parity == 0, other, own)
    result = jnp.stack([first, second], axis=2).astype(F32)
    return result.reshape(1, 1, components, count, 2 * planes * height * width)


def solution(mesh):
    placed = (P("zt", "xy", None, None, None), P("zt", "xy", None, None, None, None))
    return jax.shard_map(
        shards,
        mesh=mesh,
        in_specs=placed,
        out_specs=P("zt", "xy", None, None, None),
        check_vma=False,
    )
```

```python
import functools

import jax
import jax.numpy as jnp
from jax import lax
from jax.experimental import pallas as pl
from jax.experimental.pallas import tpu as pltpu
from jax.sharding import PartitionSpec as P

LX = 16
LY = 16
SWEEPS = 4
ROWS = 16
PAIR = 2
GROUP = 4
LANES = 128
F32 = jnp.float32
BF16 = jnp.bfloat16


def total(terms):
    while len(terms) > 1:
        terms = [sum(terms[i : i + 2][1:], terms[i]) for i in range(0, len(terms), 2)]
    return terms[0]


def multiply(blocks, vectors, partial_ref, write):
    _, count, _, _ = partial_ref.shape
    sixteens = 4

    @pl.loop(0, ROWS // PAIR)
    def _(pair):
        for first in range(0, count, GROUP):
            sums = {}
            for block, vector in zip(blocks, vectors):
                rows = [[block(pair * PAIR + o, i) for i in range(sixteens)] for o in range(PAIR)]
                for r in range(first, first + GROUP):
                    column = [vector(r, i) for i in range(sixteens)]
                    for o in range(PAIR):
                        term = total([a * v for a, v in zip(rows[o], column)])
                        term = (term[:8] + term[8:]).astype(F32)
                        sums[o, r] = sums[o, r] + term if (o, r) in sums else term
            for (o, r), value in sums.items():
                place = pl.ds(pl.multiple_of((pair * PAIR + o) * 8, 8), 8)
                partial_ref[0, r, place, :] = value[:, :LANES]
                partial_ref[1, r, place, :] = value[:, LANES:]

    for r in range(count):
        for half in range(2):
            parts = []
            for eight in range(ROWS // 8):
                parts.append(
                    total([partial_ref[half, r, pl.ds(eight * 64 + j, 8, stride=8), :] for j in range(8)])
                )
            write(r, half, jnp.concatenate(parts, axis=0))


def prepare_kernel(block_ref, off_ref, inverse_ref):
    rows, components, sites = block_ref.shape[1:]
    first = pl.program_id(0) * rows
    own = lax.broadcasted_iota(jnp.int32, (components, sites), 0)
    for o in range(rows):
        block = block_ref[0, o].astype(F32)
        here = own == first + o
        off_ref[o] = jnp.where(here, 0.0, block).astype(BF16)
        diagonal = jnp.sum(jnp.where(here, block, 0.0), axis=0, keepdims=True)
        inverse_ref[o : o + 1, :] = 1.0 / diagonal


def prepare(stencil):
    components, sites = stencil.shape[2:]
    return pl.pallas_call(
        prepare_kernel,
        grid=(components // ROWS,),
        in_specs=[pl.BlockSpec((1, ROWS, components, sites), lambda g: (0, g, 0, 0))],
        out_specs=[
            pl.BlockSpec((ROWS, components, sites), lambda g: (g, 0, 0)),
            pl.BlockSpec((ROWS, sites), lambda g: (g, 0)),
        ],
        out_shape=[
            jax.ShapeDtypeStruct((components, components, sites), BF16),
            jax.ShapeDtypeStruct((components, sites), F32),
        ],
        cost_estimate=pl.CostEstimate(flops=10**7, bytes_accessed=4 * 2**20, transcendentals=0),
        name="prepare",
    )(stencil)


def one_hot(index, size):
    column = lax.broadcasted_iota(jnp.int32, (size, size), 1)
    return jnp.where(column == index, 1.0, 0.0).astype(BF16)


def fine_order(sites):
    place = lax.broadcasted_iota(jnp.int32, (sites, sites), 0)
    u, w, g, h = place // 64, place // 16 % 4, place // 4 % 4, place % 4
    return u * 64 + g * 16 + w * 4 + h


def split_kernel(fine_ref, out_ref):
    rows, sites = fine_ref.shape
    _, _, planes, cells, _ = out_ref.shape
    unit = one_hot(lax.broadcasted_iota(jnp.int32, (sites, sites), 0), sites)
    turned = lax.dot_general(unit, fine_ref[...], (((1,), (1,)), ((), ())), preferred_element_type=F32)
    turned = turned.astype(BF16).reshape(2, planes, cells, rows)
    for half in range(2):
        out_ref[:, half] = turned


def split(fine, planes, cells):
    rows, _ = fine.shape
    return pl.pallas_call(
        split_kernel,
        out_shape=jax.ShapeDtypeStruct((2, 2, planes, cells, rows), BF16),
        name="split",
    )(fine)


def start_kernel(received_ref, inverse_ref, source_ref, iterate_ref, rounded_ref, turned_ref):
    count, components, sites = rounded_ref.shape
    half = lax.axis_index("xy") // (lax.axis_size("xy") // 2)
    order = one_hot(fine_order(sites), sites)
    turned = lax.dot_general(
        received_ref[half], order, (((0,), (0,)), ((), ())), preferred_element_type=F32
    )
    for i in range(sites // LANES):
        turned_ref[i] = turned[:, i * LANES : (i + 1) * LANES]
    inverse = inverse_ref[...]
    for r in range(count):
        source = jnp.concatenate(
            [turned_ref[i, pl.ds(r, components, stride=count), :] for i in range(sites // LANES)], axis=1
        )
        iterate = source * inverse
        source_ref[r] = source.astype(BF16)
        iterate_ref[r] = iterate
        rounded_ref[r] = iterate.astype(BF16)


def start(received, inverse):
    _, sites, rows = received.shape
    components = inverse.shape[0]
    shape = (rows // components, components, sites)
    return pl.pallas_call(
        start_kernel,
        out_shape=[jax.ShapeDtypeStruct(shape, t) for t in (BF16, F32, BF16)],
        scratch_shapes=[pltpu.VMEM((sites // LANES, rows, LANES), F32)],
        name="start",
    )(received, inverse)


def leave_kernel(rounded_ref, out_ref, mixed_ref):
    count, components, sites = rounded_ref.shape
    _, columns, cells, rows = out_ref.shape
    for r in range(count):
        value = rounded_ref[r].astype(F32)
        for i in range(sites // LANES):
            mixed_ref[i, pl.ds(r, components, stride=count), :] = value[:, i * LANES : (i + 1) * LANES]
    mixed = jnp.concatenate([mixed_ref[i].astype(BF16) for i in range(sites // LANES)], axis=1)
    order = one_hot(fine_order(sites), sites)
    turned = lax.dot_general(order, mixed, (((1,), (1,)), ((), ())), preferred_element_type=F32)
    turned = turned.astype(BF16).reshape(columns, cells, rows)
    for half in range(2):
        out_ref[half] = turned


def leave(rounded, columns):
    count, components, sites = rounded.shape
    rows = count * components
    return pl.pallas_call(
        leave_kernel,
        out_shape=jax.ShapeDtypeStruct((2, columns, sites // columns, rows), BF16),
        scratch_shapes=[pltpu.VMEM((sites // LANES, rows, LANES), F32)],
        name="leave",
    )(rounded)


def join_kernel(received_ref, out_ref):
    places = received_ref.shape[2]
    half = lax.axis_index("zt") % 2
    unit = one_hot(lax.broadcasted_iota(jnp.int32, (places, places), 0), places)
    for e in range(2):
        out_ref[:, places * e : places * (e + 1)] = lax.dot_general(
            received_ref[e, half], unit, (((0,), (0,)), ((), ())), preferred_element_type=F32
        )


def join(received):
    _, _, places, rows = received.shape
    return pl.pallas_call(
        join_kernel,
        out_shape=jax.ShapeDtypeStruct((rows, 2 * places), F32),
        name="join",
    )(received)


def local_kernel(off_ref, hops_ref, source_ref, iterate_ref, rounded_ref, inverse_ref, base_ref, near_ref, partial_ref):
    count, components, sites = rounded_ref.shape

    @pl.when(pl.program_id(0) == 0)
    def _():
        lane = lax.broadcasted_iota(jnp.int32, (components, sites), 1) % LX
        for r in range(count):
            value = rounded_ref[r].astype(F32)
            after = jnp.where(
                lane == LX - 1, pltpu.roll(value, LX - 1, 1), pltpu.roll(value, sites - 1, 1)
            )
            before = jnp.where(lane == 0, pltpu.roll(value, sites - LX + 1, 1), pltpu.roll(value, 1, 1))
            near_ref[0, r] = after.astype(BF16)
            near_ref[1, r] = before.astype(BF16)
            near_ref[2, r] = pltpu.roll(value, sites - LX, 1).astype(BF16)
            near_ref[3, r] = pltpu.roll(value, LX, 1).astype(BF16)

    def sixteen(i):
        return slice(16 * i, 16 * i + 16)

    blocks = [lambda o, i: off_ref[o, sixteen(i), :]]
    vectors = [lambda r, i: rounded_ref[r, sixteen(i), :]]
    for k in range(4):
        blocks.append(lambda o, i, k=k: hops_ref[k, o, sixteen(i), :])
        vectors.append(lambda r, i, k=k: near_ref[k, r, sixteen(i), :])

    here = pl.ds(pl.multiple_of(pl.program_id(0) * ROWS, ROWS), ROWS)

    def write(r, half, sums):
        lanes = slice(half * LANES, half * LANES + LANES)
        left = source_ref[r, :, lanes].astype(F32) - sums
        kept = iterate_ref[r, :, lanes] - rounded_ref[r, here, lanes].astype(F32)
        base_ref[r, :, lanes] = kept + left * inverse_ref[:, lanes]

    multiply(blocks, vectors, partial_ref, write)


def local(off, stencil, source, iterate, rounded, inverse):
    count, components, sites = rounded.shape
    part = pl.BlockSpec((count, ROWS, sites), lambda g: (0, g, 0))
    return pl.pallas_call(
        local_kernel,
        grid=(components // ROWS,),
        in_specs=[
            pl.BlockSpec((ROWS, components, sites), lambda g: (g, 0, 0)),
            pl.BlockSpec((pl.Element(4), pl.Element(ROWS), pl.Element(components), pl.Element(sites)),
                         lambda g: (1, g * ROWS, 0, 0)),
            part,
            part,
            pl.BlockSpec((count, components, sites), lambda g: (0, 0, 0)),
            pl.BlockSpec((ROWS, sites), lambda g: (g, 0)),
        ],
        out_specs=part,
        out_shape=jax.ShapeDtypeStruct(rounded.shape, F32),
        scratch_shapes=[
            pltpu.VMEM((4, count, components, sites), BF16),
            pltpu.VMEM((2, count, ROWS * 8, LANES), F32),
        ],
        compiler_params=pltpu.CompilerParams(vmem_limit_bytes=40 * 2**20),
        cost_estimate=pl.CostEstimate(flops=10**9, bytes_accessed=12 * 2**20, transcendentals=0),
        name="local",
    )(off, stencil, source, iterate, rounded, inverse)


def remote_kernel(last, hops_ref, z0_ref, z1_ref, t0_ref, t1_ref, base_ref, inverse_ref, *rest):
    if last:
        rounded_ref, partial_ref = rest
    else:
        iterate_ref, rounded_ref, partial_ref = rest

    def sixteen(i):
        return slice(16 * i, 16 * i + 16)

    z_odd = lax.axis_index("xy") % 2
    t_odd = lax.axis_index("zt") % 2
    blocks, vectors = [], []
    for k, ref in ((z_odd, z0_ref), (1 - z_odd, z1_ref), (2 + t_odd, t0_ref), (3 - t_odd, t1_ref)):
        blocks.append(lambda o, i, k=k: hops_ref[k, o, sixteen(i), :])
        vectors.append(lambda r, i, ref=ref: ref[r, sixteen(i), :])

    def write(r, half, sums):
        lanes = slice(half * LANES, half * LANES + LANES)
        iterate = base_ref[r, :, lanes] - sums * inverse_ref[:, lanes]
        if not last:
            iterate_ref[r, :, lanes] = iterate
        rounded_ref[r, :, lanes] = iterate.astype(BF16)

    multiply(blocks, vectors, partial_ref, write)


def remote(stencil, halos, base, inverse, last):
    count, components, sites = base.shape
    part = pl.BlockSpec((count, ROWS, sites), lambda g: (0, g, 0))
    whole = pl.BlockSpec((count, components, sites), lambda g: (0, 0, 0))
    types = [BF16] if last else [F32, BF16]
    return pl.pallas_call(
        functools.partial(remote_kernel, last),
        grid=(components // ROWS,),
        in_specs=[
            pl.BlockSpec((pl.Element(4), pl.Element(ROWS), pl.Element(components), pl.Element(sites)),
                         lambda g: (5, g * ROWS, 0, 0)),
            whole, whole, whole, whole,
            part,
            pl.BlockSpec((ROWS, sites), lambda g: (g, 0)),
        ],
        out_specs=[part for _ in types],
        out_shape=[jax.ShapeDtypeStruct(base.shape, t) for t in types],
        scratch_shapes=[pltpu.VMEM((2, count, ROWS * 8, LANES), F32)],
        compiler_params=pltpu.CompilerParams(vmem_limit_bytes=40 * 2**20),
        cost_estimate=pl.CostEstimate(flops=10**9, bytes_accessed=12 * 2**20, transcendentals=0),
        name="remote",
    )(stencil, *halos, base, inverse)


def pairs(plane, axis, first):
    count = lax.axis_size(axis)
    swaps = []
    for i in range(first, first + count, 2):
        a, b = i % count, (i + 1) % count
        swaps += [(a, b), (b, a)]
    return lax.ppermute(plane, axis, swaps)


def groups():
    columns = lax.axis_size("xy")
    return [list(range(i * columns, (i + 2) * columns)) for i in range(0, lax.axis_size("zt"), 2)]


def exchange(chunks):
    return lax.all_to_all(chunks, ("zt", "xy"), 0, 0, axis_index_groups=groups(), tiled=True)


def shards(restricted, stencil):
    columns = lax.axis_size("xy")
    planes = columns // 2
    components, count, sites = restricted.shape[2:]
    rows = components * count
    cells = sites // columns
    stencil = stencil[0, 0]
    off, inverse = prepare(stencil)

    chunks = split(restricted.reshape(rows, sites), planes, cells)
    received = exchange(chunks.reshape(2 * columns, cells, rows))
    source, iterate, rounded = start(received.reshape(2, sites, rows), inverse)
    for sweep in range(SWEEPS - 1):
        last = sweep == SWEEPS - 2
        halos = [
            pairs(rounded, "xy", 0),
            pairs(rounded, "xy", 1),
            pairs(rounded, "zt", 0),
            pairs(rounded, "zt", 1),
        ]
        base = local(off, stencil, source, iterate, rounded, inverse)
        results = remote(stencil, halos, base, inverse, last)
        if last:
            (rounded,) = results
        else:
            iterate, rounded = results

    chunks = leave(rounded, columns)
    received = exchange(chunks.reshape(2 * columns, cells, rows))
    result = join(received.reshape(2, 2, planes * cells, rows))
    return result.reshape(1, 1, components, count, sites)


def solution(mesh):
    placed = (P("zt", "xy", None, None, None), P("zt", "xy", None, None, None, None))
    return jax.shard_map(
        shards,
        mesh=mesh,
        in_specs=placed,
        out_specs=P("zt", "xy", None, None, None),
        check_vma=False,
    )
```

```python
import functools

import jax
import jax.numpy as jnp
from jax import lax
from jax.experimental import pallas as pl
from jax.experimental.pallas import tpu as pltpu
from jax.sharding import PartitionSpec as P

LX = 16
LY = 16
SWEEPS = 4
ROWS = 16
NEAR = 5
PAIR = 2
GROUP = 4
LANES = 128
F32 = jnp.float32
BF16 = jnp.bfloat16
SMALL = pltpu.CompilerParams(vmem_limit_bytes=8 * 2**20)


def total(terms):
    while len(terms) > 1:
        terms = [sum(terms[i : i + 2][1:], terms[i]) for i in range(0, len(terms), 2)]
    return terms[0]


def multiply(blocks, vectors, partial_ref, finish, arrive=None):
    _, count, _, _ = partial_ref.shape
    components = 64

    @pl.loop(0, components // ROWS)
    def _(step):
        start = pl.multiple_of(step * ROWS, ROWS)
        if arrive is not None:
            arrive(step)

        @pl.loop(0, ROWS // PAIR)
        def _(pair):
            row = start + pair * PAIR
            for first in range(0, count, GROUP):
                sums = {}
                for block, vector in zip(blocks, vectors):
                    rows = [[block(row + o, i) for i in range(components // 16)] for o in range(PAIR)]
                    for r in range(first, first + GROUP):
                        column = [vector(r, i) for i in range(components // 16)]
                        for o in range(PAIR):
                            term = total([a * v for a, v in zip(rows[o], column)])
                            term = (term[:8] + term[8:]).astype(F32)
                            sums[o, r] = sums[o, r] + term if (o, r) in sums else term
                for (o, r), value in sums.items():
                    place = pl.ds(pl.multiple_of((pair * PAIR + o) * 8, 8), 8)
                    partial_ref[0, r, place, :] = value[:, :LANES]
                    partial_ref[1, r, place, :] = value[:, LANES:]

        for r in range(count):
            for half in range(2):
                parts = []
                for eight in range(ROWS // 8):
                    parts.append(
                        total([partial_ref[half, r, pl.ds(eight * 64 + j, 8, stride=8), :] for j in range(8)])
                    )
                finish(r, pl.ds(start, ROWS), half, jnp.concatenate(parts, axis=0))


def prepare_kernel(block_ref, off_ref, inverse_ref):
    components, _, sites = off_ref.shape
    off_ref[...] = block_ref[0]

    @pl.loop(0, components // 16)
    def _(group):
        first = pl.multiple_of(group * 16, 16)
        here = lax.broadcasted_iota(jnp.int32, (16, sites), 0)
        diagonal = jnp.zeros((16, sites), F32)
        for o in range(16):
            block = block_ref[0, first + o, pl.ds(first, 16), :].astype(F32)
            diagonal = jnp.where(here == o, block, diagonal)
            off_ref[first + o, pl.ds(first, 16), :] = jnp.where(here == o, 0.0, block).astype(BF16)
        inverse_ref[pl.ds(first, 16), :] = 1.0 / diagonal


def prepare(stencil):
    _, components, _, sites = stencil.shape
    shape = (components, components, sites)
    return pl.pallas_call(
        prepare_kernel,
        grid=(1,),
        in_specs=[pl.BlockSpec((1, *shape), lambda g: (0, 0, 0, 0))],
        out_specs=[pl.BlockSpec(shape, lambda g: (0, 0, 0)), pl.BlockSpec((components, sites), lambda g: (0, 0))],
        out_shape=[jax.ShapeDtypeStruct(shape, BF16), jax.ShapeDtypeStruct((components, sites), F32)],
        compiler_params=pltpu.CompilerParams(vmem_limit_bytes=16 * 2**20),
        cost_estimate=pl.CostEstimate(flops=10**7, bytes_accessed=4 * 2**20, transcendentals=0),
        name="prepare",
    )(stencil)


def one_hot(index, size):
    column = lax.broadcasted_iota(jnp.int32, (size, size), 1)
    return jnp.where(column == index, 1.0, 0.0).astype(BF16)


def fine_order(sites):
    place = lax.broadcasted_iota(jnp.int32, (sites, sites), 0)
    u, w, g, h = place // 64, place // 16 % 4, place // 4 % 4, place % 4
    return u * 64 + g * 16 + w * 4 + h


def split_kernel(fine_ref, out_ref):
    rows, sites = fine_ref.shape
    _, _, planes, cells, _ = out_ref.shape
    unit = one_hot(lax.broadcasted_iota(jnp.int32, (sites, sites), 0), sites)
    turned = lax.dot_general(unit, fine_ref[...], (((1,), (1,)), ((), ())), preferred_element_type=F32)
    turned = turned.astype(BF16).reshape(2, planes, cells, rows)
    for half in range(2):
        out_ref[:, half] = turned


def split(fine, planes, cells):
    rows, _ = fine.shape
    return pl.pallas_call(
        split_kernel,
        out_shape=jax.ShapeDtypeStruct((2, 2, planes, cells, rows), BF16),
        compiler_params=SMALL,
        name="split",
    )(fine)


def start_kernel(received_ref, inverse_ref, source_ref, iterate_ref, rounded_ref, turned_ref):
    count, components, sites = rounded_ref.shape
    half = lax.axis_index("xy") // (lax.axis_size("xy") // 2)
    order = one_hot(fine_order(sites), sites)
    turned = lax.dot_general(
        received_ref[half], order, (((0,), (0,)), ((), ())), preferred_element_type=F32
    )
    for i in range(sites // LANES):
        turned_ref[i] = turned[:, i * LANES : (i + 1) * LANES]
    inverse = inverse_ref[...]
    for r in range(count):
        source = jnp.concatenate(
            [turned_ref[i, pl.ds(r, components, stride=count), :] for i in range(sites // LANES)], axis=1
        )
        iterate = source * inverse
        source_ref[r] = source.astype(BF16)
        iterate_ref[r] = iterate
        rounded_ref[r] = iterate.astype(BF16)


def start(received, inverse):
    _, sites, rows = received.shape
    components = inverse.shape[0]
    shape = (rows // components, components, sites)
    return pl.pallas_call(
        start_kernel,
        out_shape=[jax.ShapeDtypeStruct(shape, t) for t in (BF16, F32, BF16)],
        scratch_shapes=[pltpu.VMEM((sites // LANES, rows, LANES), F32)],
        compiler_params=SMALL,
        name="start",
    )(received, inverse)


def leave_kernel(rounded_ref, out_ref, mixed_ref):
    count, components, sites = rounded_ref.shape
    _, columns, cells, rows = out_ref.shape
    for r in range(count):
        value = rounded_ref[r].astype(F32)
        for i in range(sites // LANES):
            mixed_ref[i, pl.ds(r, components, stride=count), :] = value[:, i * LANES : (i + 1) * LANES]
    mixed = jnp.concatenate([mixed_ref[i].astype(BF16) for i in range(sites // LANES)], axis=1)
    order = one_hot(fine_order(sites), sites)
    turned = lax.dot_general(order, mixed, (((1,), (1,)), ((), ())), preferred_element_type=F32)
    turned = turned.astype(BF16).reshape(columns, cells, rows)
    for half in range(2):
        out_ref[half] = turned


def leave(rounded, columns):
    count, components, sites = rounded.shape
    rows = count * components
    return pl.pallas_call(
        leave_kernel,
        out_shape=jax.ShapeDtypeStruct((2, columns, sites // columns, rows), BF16),
        scratch_shapes=[pltpu.VMEM((sites // LANES, rows, LANES), F32)],
        compiler_params=SMALL,
        name="leave",
    )(rounded)


def join_kernel(received_ref, out_ref):
    places = received_ref.shape[2]
    half = lax.axis_index("zt") % 2
    unit = one_hot(lax.broadcasted_iota(jnp.int32, (places, places), 0), places)
    for e in range(2):
        out_ref[:, places * e : places * (e + 1)] = lax.dot_general(
            received_ref[e, half], unit, (((0,), (0,)), ((), ())), preferred_element_type=F32
        )


def join(received):
    _, _, places, rows = received.shape
    return pl.pallas_call(
        join_kernel,
        out_shape=jax.ShapeDtypeStruct((rows, 2 * places), F32),
        compiler_params=SMALL,
        name="join",
    )(received)


def sixteen(i):
    return slice(16 * i, 16 * i + 16)


def lanes(half):
    return slice(half * LANES, half * LANES + LANES)


def loads(pieces, kept_ref, sems):
    copies = []
    for step in range(kept_ref.shape[1] // ROWS):
        rows = pl.ds(step * ROWS, ROWS)
        for piece, (source, there, here, terms) in enumerate(pieces):
            from_ref = source.at[pl.ds(there, terms), rows]
            copies.append(
                pltpu.make_async_copy(from_ref, kept_ref.at[pl.ds(here, terms), rows], sems.at[piece, step])
            )
    return copies


def arrival(pieces, kept_ref, sems):
    def arrive(step):
        rows = pl.ds(pl.multiple_of(step * ROWS, ROWS), ROWS)
        for piece, (source, there, here, terms) in enumerate(pieces):
            from_ref = source.at[pl.ds(there, terms), rows]
            pltpu.make_async_copy(from_ref, kept_ref.at[pl.ds(here, terms), rows], sems.at[piece, step]).wait()

    return arrive


def local_kernel(first, *refs):
    if first:
        off_ref, far_ref, source_ref, iterate_ref, rounded_ref, inverse_ref = refs[:6]
        base_ref, stencil_ref, near_ref, partial_ref, sems = refs[6:]
        pieces = [(off_ref, 0, 0, 1), (far_ref, 1, 1, NEAR - 1)]
        for copy in loads(pieces, stencil_ref, sems):
            copy.start()
        arrive = arrival(pieces, stencil_ref, sems)
    else:
        stencil_ref, source_ref, iterate_ref, rounded_ref, inverse_ref, base_ref, near_ref, partial_ref = refs
        arrive = None
    count, components, sites = rounded_ref.shape
    lane = lax.broadcasted_iota(jnp.int32, (components, sites), 1) % LX

    @pl.loop(0, count)
    def _(r):
        value = rounded_ref[r].astype(F32)
        after = jnp.where(lane == LX - 1, pltpu.roll(value, LX - 1, 1), pltpu.roll(value, sites - 1, 1))
        before = jnp.where(lane == 0, pltpu.roll(value, sites - LX + 1, 1), pltpu.roll(value, 1, 1))
        near_ref[0, r] = after.astype(BF16)
        near_ref[1, r] = before.astype(BF16)
        near_ref[2, r] = pltpu.roll(value, sites - LX, 1).astype(BF16)
        near_ref[3, r] = pltpu.roll(value, LX, 1).astype(BF16)

    blocks = [lambda o, i, k=k: stencil_ref[k, o, sixteen(i), :] for k in range(NEAR)]
    vectors = [lambda r, i: rounded_ref[r, sixteen(i), :]]
    for k in range(NEAR - 1):
        vectors.append(lambda r, i, k=k: near_ref[k, r, sixteen(i), :])

    def finish(r, rows, half, sums):
        part = lanes(half)
        left = source_ref[r, rows, part].astype(F32) - sums
        kept = iterate_ref[r, rows, part] - rounded_ref[r, rows, part].astype(F32)
        base_ref[r, rows, part] = kept + left * inverse_ref[rows, part]

    multiply(blocks, vectors, partial_ref, finish, arrive)


def vmem(count):
    return [pl.BlockSpec(memory_space=pltpu.VMEM)] * count


def hbm(count):
    return [pl.BlockSpec(memory_space=pltpu.HBM)] * count


def local(stencil, source, iterate, rounded, inverse):
    count, components, sites = rounded.shape
    first = isinstance(stencil, tuple)
    kept = (NEAR, components, components, sites)
    scratch = [
        pltpu.VMEM((4, count, components, sites), BF16),
        pltpu.VMEM((2, count, ROWS * 8, LANES), F32),
    ]
    if first:
        scratch.append(pltpu.SemaphoreType.DMA((2, components // ROWS)))
    base = jax.ShapeDtypeStruct(rounded.shape, F32)
    blocks = stencil if first else (stencil,)
    return pl.pallas_call(
        functools.partial(local_kernel, first),
        in_specs=(hbm(2) if first else vmem(1)) + vmem(4),
        out_specs=vmem(2) if first else vmem(1)[0],
        out_shape=[base, pltpu.VMEM(kept, BF16)] if first else base,
        scratch_shapes=scratch,
        compiler_params=SMALL,
        cost_estimate=pl.CostEstimate(flops=10**9, bytes_accessed=12 * 2**20, transcendentals=0),
        name="local",
    )(*blocks, source, iterate, rounded, inverse)


def remote_kernel(first, last, *refs):
    if first:
        whole_ref, z0_ref, z1_ref, t0_ref, t1_ref, base_ref, inverse_ref = refs[:7]
        iterate_ref, rounded_ref, stencil_ref, partial_ref, sems = refs[7:]
        pieces = [(whole_ref, NEAR, 0, stencil_ref.shape[0])]
        for copy in loads(pieces, stencil_ref, sems):
            copy.start()
        arrive = arrival(pieces, stencil_ref, sems)
    else:
        stencil_ref, z0_ref, z1_ref, t0_ref, t1_ref, base_ref, inverse_ref = refs[:7]
        if last:
            rounded_ref, partial_ref = refs[7:]
        else:
            iterate_ref, rounded_ref, partial_ref = refs[7:]
        arrive = None

    z_odd = lax.axis_index("xy") % 2
    t_odd = lax.axis_index("zt") % 2
    blocks, vectors = [], []
    for k, ref in ((z_odd, z0_ref), (1 - z_odd, z1_ref), (2 + t_odd, t0_ref), (3 - t_odd, t1_ref)):
        blocks.append(lambda o, i, k=k: stencil_ref[k, o, sixteen(i), :])
        vectors.append(lambda r, i, ref=ref: ref[r, sixteen(i), :])

    def finish(r, rows, half, sums):
        part = lanes(half)
        iterate = base_ref[r, rows, part] - sums * inverse_ref[rows, part]
        if not last:
            iterate_ref[r, rows, part] = iterate
        rounded_ref[r, rows, part] = iterate.astype(BF16)

    multiply(blocks, vectors, partial_ref, finish, arrive)


def remote(stencil, halos, base, inverse, first, last):
    count, components, sites = base.shape
    types = [BF16] if last else [F32, BF16]
    shapes = [jax.ShapeDtypeStruct(base.shape, t) for t in types]
    scratch = [pltpu.VMEM((2, count, ROWS * 8, LANES), F32)]
    if first:
        shapes.append(pltpu.VMEM((stencil.shape[0] - NEAR, components, components, sites), BF16))
        scratch.append(pltpu.SemaphoreType.DMA((1, components // ROWS)))
    return pl.pallas_call(
        functools.partial(remote_kernel, first, last),
        in_specs=(hbm(1) if first else vmem(1)) + vmem(6),
        out_specs=vmem(len(shapes)),
        out_shape=shapes,
        scratch_shapes=scratch,
        compiler_params=SMALL,
        cost_estimate=pl.CostEstimate(flops=10**9, bytes_accessed=12 * 2**20, transcendentals=0),
        name="remote",
    )(stencil, *halos, base, inverse)


def pairs(plane, axis, first):
    count = lax.axis_size(axis)
    swaps = []
    for i in range(first, first + count, 2):
        a, b = i % count, (i + 1) % count
        swaps += [(a, b), (b, a)]
    return lax.ppermute(plane, axis, swaps)


def groups():
    columns = lax.axis_size("xy")
    return [list(range(i * columns, (i + 2) * columns)) for i in range(0, lax.axis_size("zt"), 2)]


def exchange(chunks):
    return lax.all_to_all(chunks, ("zt", "xy"), 0, 0, axis_index_groups=groups(), tiled=True)


def shards(restricted, stencil):
    columns = lax.axis_size("xy")
    planes = columns // 2
    components, count, sites = restricted.shape[2:]
    rows = components * count
    cells = sites // columns
    stencil = pltpu.with_memory_space_constraint(stencil[0, 0], pltpu.HBM)
    off, inverse = prepare(stencil)

    chunks = split(restricted.reshape(rows, sites), planes, cells)
    received = exchange(chunks.reshape(2 * columns, cells, rows))
    source, iterate, rounded = start(received.reshape(2, sites, rows), inverse)
    for sweep in range(SWEEPS - 1):
        last = sweep == SWEEPS - 2
        halos = [
            pairs(rounded, "xy", 0),
            pairs(rounded, "xy", 1),
            pairs(rounded, "zt", 0),
            pairs(rounded, "zt", 1),
        ]
        if sweep == 0:
            base, near = local((off[None], stencil), source, iterate, rounded, inverse)
            iterate, rounded, far = remote(stencil, halos, base, inverse, True, False)
        elif not last:
            base = local(near, source, iterate, rounded, inverse)
            iterate, rounded = remote(far, halos, base, inverse, False, False)
        else:
            base = local(near, source, iterate, rounded, inverse)
            (rounded,) = remote(far, halos, base, inverse, False, True)

    chunks = leave(rounded, columns)
    received = exchange(chunks.reshape(2 * columns, cells, rows))
    result = join(received.reshape(2, 2, planes * cells, rows))
    return result.reshape(1, 1, components, count, sites)


def solution(mesh):
    placed = (P("zt", "xy", None, None, None), P("zt", "xy", None, None, None, None))
    return jax.shard_map(
        shards,
        mesh=mesh,
        in_specs=placed,
        out_specs=P("zt", "xy", None, None, None),
        check_vma=False,
    )
```

```python
import functools

import jax
import jax.numpy as jnp
from jax import lax
from jax.experimental import pallas as pl
from jax.experimental.pallas import tpu as pltpu
from jax.sharding import PartitionSpec as P

LX = 16
LY = 16
SWEEPS = 4
ROWS = 16
NEAR = 5
PAIR = 1
GROUP = 8
TERMS = 2
LANES = 128
F32 = jnp.float32
BF16 = jnp.bfloat16
SMALL = pltpu.CompilerParams(vmem_limit_bytes=8 * 2**20)


def total(terms):
    while len(terms) > 1:
        terms = [sum(terms[i : i + 2][1:], terms[i]) for i in range(0, len(terms), 2)]
    return terms[0]


def multiply(blocks, vectors, partial_ref, finish, arrive=None):
    _, count, _, _ = partial_ref.shape
    components = 64

    @pl.loop(0, components // ROWS)
    def _(step):
        start = pl.multiple_of(step * ROWS, ROWS)
        if arrive is not None:
            arrive(step)

        @pl.loop(0, ROWS // PAIR)
        def _(pair):
            row = start + pair * PAIR
            for first in range(0, count, GROUP):
                sums = {}
                for k in range(0, len(blocks), TERMS):
                    some = list(zip(blocks, vectors))[k : k + TERMS]
                    rows = [
                        [block(row + o, i) for block, _ in some for i in range(components // 16)] for o in range(PAIR)
                    ]
                    for r in range(first, first + GROUP):
                        column = [vector(r, i) for _, vector in some for i in range(components // 16)]
                        for o in range(PAIR):
                            term = total([a * v for a, v in zip(rows[o], column)])
                            term = (term[:8] + term[8:]).astype(F32)
                            sums[o, r] = sums[o, r] + term if (o, r) in sums else term
                for (o, r), value in sums.items():
                    place = pl.ds(pl.multiple_of((pair * PAIR + o) * 8, 8), 8)
                    partial_ref[0, r, place, :] = value[:, :LANES]
                    partial_ref[1, r, place, :] = value[:, LANES:]

        for r in range(count):
            for half in range(2):
                parts = []
                for eight in range(ROWS // 8):
                    parts.append(
                        total([partial_ref[half, r, pl.ds(eight * 64 + j, 8, stride=8), :] for j in range(8)])
                    )
                finish(r, pl.ds(start, ROWS), half, jnp.concatenate(parts, axis=0))


def prepare_kernel(block_ref, off_ref, inverse_ref):
    components, _, sites = off_ref.shape
    off_ref[...] = block_ref[0]

    @pl.loop(0, components // 16)
    def _(group):
        first = pl.multiple_of(group * 16, 16)
        here = lax.broadcasted_iota(jnp.int32, (16, sites), 0)
        diagonal = jnp.zeros((16, sites), F32)
        for o in range(16):
            block = block_ref[0, first + o, pl.ds(first, 16), :].astype(F32)
            diagonal = jnp.where(here == o, block, diagonal)
            off_ref[first + o, pl.ds(first, 16), :] = jnp.where(here == o, 0.0, block).astype(BF16)
        inverse_ref[pl.ds(first, 16), :] = 1.0 / diagonal


def prepare(stencil):
    _, components, _, sites = stencil.shape
    shape = (components, components, sites)
    return pl.pallas_call(
        prepare_kernel,
        grid=(1,),
        in_specs=[pl.BlockSpec((1, *shape), lambda g: (0, 0, 0, 0))],
        out_specs=[pl.BlockSpec(shape, lambda g: (0, 0, 0)), pl.BlockSpec((components, sites), lambda g: (0, 0))],
        out_shape=[jax.ShapeDtypeStruct(shape, BF16), jax.ShapeDtypeStruct((components, sites), F32)],
        compiler_params=pltpu.CompilerParams(vmem_limit_bytes=16 * 2**20),
        cost_estimate=pl.CostEstimate(flops=10**7, bytes_accessed=4 * 2**20, transcendentals=0),
        name="prepare",
    )(stencil)


def one_hot(index, size):
    column = lax.broadcasted_iota(jnp.int32, (size, size), 1)
    return jnp.where(column == index, 1.0, 0.0).astype(BF16)


def fine_order(sites):
    place = lax.broadcasted_iota(jnp.int32, (sites, sites), 0)
    u, w, g, h = place // 64, place // 16 % 4, place // 4 % 4, place % 4
    return u * 64 + g * 16 + w * 4 + h


def split_kernel(fine_ref, out_ref):
    rows, sites = fine_ref.shape
    _, _, planes, cells, _ = out_ref.shape
    unit = one_hot(lax.broadcasted_iota(jnp.int32, (sites, sites), 0), sites)
    turned = lax.dot_general(unit, fine_ref[...], (((1,), (1,)), ((), ())), preferred_element_type=F32)
    turned = turned.astype(BF16).reshape(2, planes, cells, rows)
    for half in range(2):
        out_ref[:, half] = turned


def split(fine, planes, cells):
    rows, _ = fine.shape
    return pl.pallas_call(
        split_kernel,
        out_shape=jax.ShapeDtypeStruct((2, 2, planes, cells, rows), BF16),
        compiler_params=SMALL,
        name="split",
    )(fine)


def start_kernel(received_ref, inverse_ref, source_ref, iterate_ref, rounded_ref, turned_ref):
    count, components, sites = rounded_ref.shape
    half = lax.axis_index("xy") // (lax.axis_size("xy") // 2)
    order = one_hot(fine_order(sites), sites)
    turned = lax.dot_general(
        received_ref[half], order, (((0,), (0,)), ((), ())), preferred_element_type=F32
    )
    for i in range(sites // LANES):
        turned_ref[i] = turned[:, i * LANES : (i + 1) * LANES]
    inverse = inverse_ref[...]
    for r in range(count):
        source = jnp.concatenate(
            [turned_ref[i, pl.ds(r, components, stride=count), :] for i in range(sites // LANES)], axis=1
        )
        iterate = source * inverse
        source_ref[r] = source.astype(BF16)
        iterate_ref[r] = iterate
        rounded_ref[r] = iterate.astype(BF16)


def start(received, inverse):
    _, sites, rows = received.shape
    components = inverse.shape[0]
    shape = (rows // components, components, sites)
    return pl.pallas_call(
        start_kernel,
        out_shape=[jax.ShapeDtypeStruct(shape, t) for t in (BF16, F32, BF16)],
        scratch_shapes=[pltpu.VMEM((sites // LANES, rows, LANES), F32)],
        compiler_params=SMALL,
        name="start",
    )(received, inverse)


def leave_kernel(rounded_ref, out_ref, mixed_ref):
    count, components, sites = rounded_ref.shape
    _, columns, cells, rows = out_ref.shape
    for r in range(count):
        value = rounded_ref[r].astype(F32)
        for i in range(sites // LANES):
            mixed_ref[i, pl.ds(r, components, stride=count), :] = value[:, i * LANES : (i + 1) * LANES]
    mixed = jnp.concatenate([mixed_ref[i].astype(BF16) for i in range(sites // LANES)], axis=1)
    order = one_hot(fine_order(sites), sites)
    turned = lax.dot_general(order, mixed, (((1,), (1,)), ((), ())), preferred_element_type=F32)
    turned = turned.astype(BF16).reshape(columns, cells, rows)
    for half in range(2):
        out_ref[half] = turned


def leave(rounded, columns):
    count, components, sites = rounded.shape
    rows = count * components
    return pl.pallas_call(
        leave_kernel,
        out_shape=jax.ShapeDtypeStruct((2, columns, sites // columns, rows), BF16),
        scratch_shapes=[pltpu.VMEM((sites // LANES, rows, LANES), F32)],
        compiler_params=SMALL,
        name="leave",
    )(rounded)


def join_kernel(received_ref, out_ref):
    places = received_ref.shape[2]
    half = lax.axis_index("zt") % 2
    unit = one_hot(lax.broadcasted_iota(jnp.int32, (places, places), 0), places)
    for e in range(2):
        out_ref[:, places * e : places * (e + 1)] = lax.dot_general(
            received_ref[e, half], unit, (((0,), (0,)), ((), ())), preferred_element_type=F32
        )


def join(received):
    _, _, places, rows = received.shape
    return pl.pallas_call(
        join_kernel,
        out_shape=jax.ShapeDtypeStruct((rows, 2 * places), F32),
        compiler_params=SMALL,
        name="join",
    )(received)


def sixteen(i):
    return slice(16 * i, 16 * i + 16)


def lanes(half):
    return slice(half * LANES, half * LANES + LANES)


def loads(pieces, kept_ref, sems):
    copies = []
    for step in range(kept_ref.shape[1] // ROWS):
        rows = pl.ds(step * ROWS, ROWS)
        for piece, (source, there, here, terms) in enumerate(pieces):
            from_ref = source.at[pl.ds(there, terms), rows]
            copies.append(
                pltpu.make_async_copy(from_ref, kept_ref.at[pl.ds(here, terms), rows], sems.at[piece, step])
            )
    return copies


def arrival(pieces, kept_ref, sems):
    def arrive(step):
        rows = pl.ds(pl.multiple_of(step * ROWS, ROWS), ROWS)
        for piece, (source, there, here, terms) in enumerate(pieces):
            from_ref = source.at[pl.ds(there, terms), rows]
            pltpu.make_async_copy(from_ref, kept_ref.at[pl.ds(here, terms), rows], sems.at[piece, step]).wait()

    return arrive


def local_kernel(first, *refs):
    if first:
        off_ref, far_ref, source_ref, iterate_ref, rounded_ref, inverse_ref = refs[:6]
        base_ref, stencil_ref, near_ref, partial_ref, sems = refs[6:]
        pieces = [(off_ref, 0, 0, 1), (far_ref, 1, 1, NEAR - 1)]
        for copy in loads(pieces, stencil_ref, sems):
            copy.start()
        arrive = arrival(pieces, stencil_ref, sems)
    else:
        stencil_ref, source_ref, iterate_ref, rounded_ref, inverse_ref, base_ref, near_ref, partial_ref = refs
        arrive = None
    count, components, sites = rounded_ref.shape
    lane = lax.broadcasted_iota(jnp.int32, (components, sites), 1) % LX

    @pl.loop(0, count)
    def _(r):
        value = rounded_ref[r].astype(F32)
        after = jnp.where(lane == LX - 1, pltpu.roll(value, LX - 1, 1), pltpu.roll(value, sites - 1, 1))
        before = jnp.where(lane == 0, pltpu.roll(value, sites - LX + 1, 1), pltpu.roll(value, 1, 1))
        near_ref[0, r] = after.astype(BF16)
        near_ref[1, r] = before.astype(BF16)
        near_ref[2, r] = pltpu.roll(value, sites - LX, 1).astype(BF16)
        near_ref[3, r] = pltpu.roll(value, LX, 1).astype(BF16)

    blocks = [lambda o, i, k=k: stencil_ref[k, o, sixteen(i), :] for k in range(NEAR)]
    vectors = [lambda r, i: rounded_ref[r, sixteen(i), :]]
    for k in range(NEAR - 1):
        vectors.append(lambda r, i, k=k: near_ref[k, r, sixteen(i), :])

    def finish(r, rows, half, sums):
        part = lanes(half)
        left = source_ref[r, rows, part].astype(F32) - sums
        kept = iterate_ref[r, rows, part] - rounded_ref[r, rows, part].astype(F32)
        base_ref[r, rows, part] = kept + left * inverse_ref[rows, part]

    multiply(blocks, vectors, partial_ref, finish, arrive)


def vmem(count):
    return [pl.BlockSpec(memory_space=pltpu.VMEM)] * count


def hbm(count):
    return [pl.BlockSpec(memory_space=pltpu.HBM)] * count


def local(stencil, source, iterate, rounded, inverse):
    count, components, sites = rounded.shape
    first = isinstance(stencil, tuple)
    kept = (NEAR, components, components, sites)
    scratch = [
        pltpu.VMEM((4, count, components, sites), BF16),
        pltpu.VMEM((2, count, ROWS * 8, LANES), F32),
    ]
    if first:
        scratch.append(pltpu.SemaphoreType.DMA((2, components // ROWS)))
    base = jax.ShapeDtypeStruct(rounded.shape, F32)
    blocks = stencil if first else (stencil,)
    return pl.pallas_call(
        functools.partial(local_kernel, first),
        in_specs=(hbm(2) if first else vmem(1)) + vmem(4),
        out_specs=vmem(2) if first else vmem(1)[0],
        out_shape=[base, pltpu.VMEM(kept, BF16)] if first else base,
        scratch_shapes=scratch,
        compiler_params=SMALL,
        cost_estimate=pl.CostEstimate(flops=10**9, bytes_accessed=12 * 2**20, transcendentals=0),
        name="local",
    )(*blocks, source, iterate, rounded, inverse)


def remote_kernel(first, last, *refs):
    if first:
        whole_ref, z0_ref, z1_ref, t0_ref, t1_ref, base_ref, inverse_ref = refs[:7]
        iterate_ref, rounded_ref, stencil_ref, partial_ref, sems = refs[7:]
        pieces = [(whole_ref, NEAR, 0, stencil_ref.shape[0])]
        for copy in loads(pieces, stencil_ref, sems):
            copy.start()
        arrive = arrival(pieces, stencil_ref, sems)
    else:
        stencil_ref, z0_ref, z1_ref, t0_ref, t1_ref, base_ref, inverse_ref = refs[:7]
        if last:
            rounded_ref, partial_ref = refs[7:]
        else:
            iterate_ref, rounded_ref, partial_ref = refs[7:]
        arrive = None

    z_odd = lax.axis_index("xy") % 2
    t_odd = lax.axis_index("zt") % 2
    blocks, vectors = [], []
    for k, ref in ((z_odd, z0_ref), (1 - z_odd, z1_ref), (2 + t_odd, t0_ref), (3 - t_odd, t1_ref)):
        blocks.append(lambda o, i, k=k: stencil_ref[k, o, sixteen(i), :])
        vectors.append(lambda r, i, ref=ref: ref[r, sixteen(i), :])

    def finish(r, rows, half, sums):
        part = lanes(half)
        iterate = base_ref[r, rows, part] - sums * inverse_ref[rows, part]
        if not last:
            iterate_ref[r, rows, part] = iterate
        rounded_ref[r, rows, part] = iterate.astype(BF16)

    multiply(blocks, vectors, partial_ref, finish, arrive)


def remote(stencil, halos, base, inverse, first, last):
    count, components, sites = base.shape
    types = [BF16] if last else [F32, BF16]
    shapes = [jax.ShapeDtypeStruct(base.shape, t) for t in types]
    scratch = [pltpu.VMEM((2, count, ROWS * 8, LANES), F32)]
    if first:
        shapes.append(pltpu.VMEM((stencil.shape[0] - NEAR, components, components, sites), BF16))
        scratch.append(pltpu.SemaphoreType.DMA((1, components // ROWS)))
    return pl.pallas_call(
        functools.partial(remote_kernel, first, last),
        in_specs=(hbm(1) if first else vmem(1)) + vmem(6),
        out_specs=vmem(len(shapes)),
        out_shape=shapes,
        scratch_shapes=scratch,
        compiler_params=SMALL,
        cost_estimate=pl.CostEstimate(flops=10**9, bytes_accessed=12 * 2**20, transcendentals=0),
        name="remote",
    )(stencil, *halos, base, inverse)


def pairs(plane, axis, first):
    count = lax.axis_size(axis)
    swaps = []
    for i in range(first, first + count, 2):
        a, b = i % count, (i + 1) % count
        swaps += [(a, b), (b, a)]
    return lax.ppermute(plane, axis, swaps)


def groups():
    columns = lax.axis_size("xy")
    return [list(range(i * columns, (i + 2) * columns)) for i in range(0, lax.axis_size("zt"), 2)]


def exchange(chunks):
    return lax.all_to_all(chunks, ("zt", "xy"), 0, 0, axis_index_groups=groups(), tiled=True)


def shards(restricted, stencil):
    columns = lax.axis_size("xy")
    planes = columns // 2
    components, count, sites = restricted.shape[2:]
    rows = components * count
    cells = sites // columns
    stencil = pltpu.with_memory_space_constraint(stencil[0, 0], pltpu.HBM)
    off, inverse = prepare(stencil)

    chunks = split(restricted.reshape(rows, sites), planes, cells)
    received = exchange(chunks.reshape(2 * columns, cells, rows))
    source, iterate, rounded = start(received.reshape(2, sites, rows), inverse)
    for sweep in range(SWEEPS - 1):
        last = sweep == SWEEPS - 2
        halos = [
            pairs(rounded, "xy", 0),
            pairs(rounded, "xy", 1),
            pairs(rounded, "zt", 0),
            pairs(rounded, "zt", 1),
        ]
        if sweep == 0:
            base, near = local((off[None], stencil), source, iterate, rounded, inverse)
            iterate, rounded, far = remote(stencil, halos, base, inverse, True, False)
        elif not last:
            base = local(near, source, iterate, rounded, inverse)
            iterate, rounded = remote(far, halos, base, inverse, False, False)
        else:
            base = local(near, source, iterate, rounded, inverse)
            (rounded,) = remote(far, halos, base, inverse, False, True)

    chunks = leave(rounded, columns)
    received = exchange(chunks.reshape(2 * columns, cells, rows))
    result = join(received.reshape(2, 2, planes * cells, rows))
    return result.reshape(1, 1, components, count, sites)


def solution(mesh):
    placed = (P("zt", "xy", None, None, None), P("zt", "xy", None, None, None, None))
    return jax.shard_map(
        shards,
        mesh=mesh,
        in_specs=placed,
        out_specs=P("zt", "xy", None, None, None),
        check_vma=False,
    )
```

```python
import functools

import jax
import jax.numpy as jnp
from jax import lax
from jax.experimental import pallas as pl
from jax.experimental.pallas import tpu as pltpu
from jax.sharding import PartitionSpec as P

LX = 16
LY = 16
SWEEPS = 4
ROWS = 16
NEAR = 5
PAIR = 1
GROUP = 8
TERMS = 2
LANES = 128
F32 = jnp.float32
BF16 = jnp.bfloat16
SMALL = pltpu.CompilerParams(vmem_limit_bytes=8 * 2**20)


def total(terms):
    while len(terms) > 1:
        terms = [sum(terms[i : i + 2][1:], terms[i]) for i in range(0, len(terms), 2)]
    return terms[0]


def multiply(blocks, vectors, partial_ref, finish, arrive=None):
    _, count, _, _ = partial_ref.shape
    components = 64

    @pl.loop(0, components // ROWS)
    def _(step):
        start = pl.multiple_of(step * ROWS, ROWS)
        if arrive is not None:
            arrive(step)

        @pl.loop(0, ROWS // PAIR, unroll=4)
        def _(pair):
            row = start + pair * PAIR
            for first in range(0, count, GROUP):
                sums = {}
                for k in range(0, len(blocks), TERMS):
                    some = list(zip(blocks, vectors))[k : k + TERMS]
                    rows = [
                        [block(row + o, i) for block, _ in some for i in range(components // 16)] for o in range(PAIR)
                    ]
                    for r in range(first, first + GROUP):
                        column = [vector(r, i) for _, vector in some for i in range(components // 16)]
                        for o in range(PAIR):
                            term = total([a * v for a, v in zip(rows[o], column)])
                            term = (term[:8] + term[8:]).astype(F32)
                            sums[o, r] = sums[o, r] + term if (o, r) in sums else term
                for (o, r), value in sums.items():
                    place = pl.ds(pl.multiple_of((pair * PAIR + o) * 8, 8), 8)
                    partial_ref[0, r, place, :] = value[:, :LANES]
                    partial_ref[1, r, place, :] = value[:, LANES:]

        for r in range(count):
            sums = [
                [
                    total([partial_ref[half, r, pl.ds(eight * 64 + j, 8, stride=8), :] for j in range(8)])
                    for half in range(2)
                ]
                for eight in range(ROWS // 8)
            ]
            sums = jnp.concatenate([jnp.concatenate(halves, axis=1) for halves in sums], axis=0)
            finish(r, pl.ds(start, ROWS), sums)


def prepare_kernel(block_ref, off_ref, inverse_ref):
    components, _, sites = off_ref.shape
    off_ref[...] = block_ref[0]

    @pl.loop(0, components // 16)
    def _(group):
        first = pl.multiple_of(group * 16, 16)
        here = lax.broadcasted_iota(jnp.int32, (16, sites), 0)
        diagonal = jnp.zeros((16, sites), F32)
        for o in range(16):
            block = block_ref[0, first + o, pl.ds(first, 16), :].astype(F32)
            diagonal = jnp.where(here == o, block, diagonal)
            off_ref[first + o, pl.ds(first, 16), :] = jnp.where(here == o, 0.0, block).astype(BF16)
        inverse_ref[pl.ds(first, 16), :] = 1.0 / diagonal


def prepare(stencil):
    _, components, _, sites = stencil.shape
    shape = (components, components, sites)
    return pl.pallas_call(
        prepare_kernel,
        grid=(1,),
        in_specs=[pl.BlockSpec((1, *shape), lambda g: (0, 0, 0, 0))],
        out_specs=[pl.BlockSpec(shape, lambda g: (0, 0, 0)), pl.BlockSpec((components, sites), lambda g: (0, 0))],
        out_shape=[jax.ShapeDtypeStruct(shape, BF16), jax.ShapeDtypeStruct((components, sites), F32)],
        compiler_params=pltpu.CompilerParams(vmem_limit_bytes=16 * 2**20),
        cost_estimate=pl.CostEstimate(flops=10**7, bytes_accessed=4 * 2**20, transcendentals=0),
        name="prepare",
    )(stencil)


def one_hot(index, size):
    column = lax.broadcasted_iota(jnp.int32, (size, size), 1)
    return jnp.where(column == index, 1.0, 0.0).astype(BF16)


def fine_order(sites):
    place = lax.broadcasted_iota(jnp.int32, (sites, sites), 0)
    u, w, g, h = place // 64, place // 16 % 4, place // 4 % 4, place % 4
    return u * 64 + g * 16 + w * 4 + h


def split_kernel(fine_ref, out_ref):
    rows, sites = fine_ref.shape
    _, _, planes, cells, _ = out_ref.shape
    unit = one_hot(lax.broadcasted_iota(jnp.int32, (sites, sites), 0), sites)
    turned = lax.dot_general(unit, fine_ref[...], (((1,), (1,)), ((), ())), preferred_element_type=F32)
    turned = turned.astype(BF16).reshape(2, planes, cells, rows)
    for half in range(2):
        out_ref[:, half] = turned


def split(fine, planes, cells):
    rows, _ = fine.shape
    return pl.pallas_call(
        split_kernel,
        out_shape=jax.ShapeDtypeStruct((2, 2, planes, cells, rows), BF16),
        compiler_params=SMALL,
        name="split",
    )(fine)


def start_kernel(received_ref, inverse_ref, source_ref, iterate_ref, rounded_ref, turned_ref):
    count, components, sites = rounded_ref.shape
    half = lax.axis_index("xy") // (lax.axis_size("xy") // 2)
    order = one_hot(fine_order(sites), sites)
    turned = lax.dot_general(
        received_ref[half], order, (((0,), (0,)), ((), ())), preferred_element_type=F32
    )
    for i in range(sites // LANES):
        turned_ref[i] = turned[:, i * LANES : (i + 1) * LANES]
    inverse = inverse_ref[...]
    for r in range(count):
        source = jnp.concatenate(
            [turned_ref[i, pl.ds(r, components, stride=count), :] for i in range(sites // LANES)], axis=1
        )
        iterate = source * inverse
        source_ref[r] = source.astype(BF16)
        iterate_ref[r] = iterate
        rounded_ref[r] = iterate.astype(BF16)


def start(received, inverse):
    _, sites, rows = received.shape
    components = inverse.shape[0]
    shape = (rows // components, components, sites)
    return pl.pallas_call(
        start_kernel,
        out_shape=[jax.ShapeDtypeStruct(shape, t) for t in (BF16, F32, BF16)],
        scratch_shapes=[pltpu.VMEM((sites // LANES, rows, LANES), F32)],
        compiler_params=SMALL,
        name="start",
    )(received, inverse)


def leave_kernel(rounded_ref, out_ref, mixed_ref):
    count, components, sites = rounded_ref.shape
    _, columns, cells, rows = out_ref.shape
    for r in range(count):
        value = rounded_ref[r].astype(F32)
        for i in range(sites // LANES):
            mixed_ref[i, pl.ds(r, components, stride=count), :] = value[:, i * LANES : (i + 1) * LANES]
    mixed = jnp.concatenate([mixed_ref[i].astype(BF16) for i in range(sites // LANES)], axis=1)
    order = one_hot(fine_order(sites), sites)
    turned = lax.dot_general(order, mixed, (((1,), (1,)), ((), ())), preferred_element_type=F32)
    turned = turned.astype(BF16).reshape(columns, cells, rows)
    for half in range(2):
        out_ref[half] = turned


def leave(rounded, columns):
    count, components, sites = rounded.shape
    rows = count * components
    return pl.pallas_call(
        leave_kernel,
        out_shape=jax.ShapeDtypeStruct((2, columns, sites // columns, rows), BF16),
        scratch_shapes=[pltpu.VMEM((sites // LANES, rows, LANES), F32)],
        compiler_params=SMALL,
        name="leave",
    )(rounded)


def join_kernel(received_ref, out_ref):
    places = received_ref.shape[2]
    half = lax.axis_index("zt") % 2
    unit = one_hot(lax.broadcasted_iota(jnp.int32, (places, places), 0), places)
    for e in range(2):
        out_ref[:, places * e : places * (e + 1)] = lax.dot_general(
            received_ref[e, half], unit, (((0,), (0,)), ((), ())), preferred_element_type=F32
        )


def join(received):
    _, _, places, rows = received.shape
    return pl.pallas_call(
        join_kernel,
        out_shape=jax.ShapeDtypeStruct((rows, 2 * places), F32),
        compiler_params=SMALL,
        name="join",
    )(received)


def sixteen(i):
    return slice(16 * i, 16 * i + 16)


def loads(pieces, kept_ref, sems):
    copies = []
    for step in range(kept_ref.shape[1] // ROWS):
        rows = pl.ds(step * ROWS, ROWS)
        for piece, (source, there, here, terms) in enumerate(pieces):
            from_ref = source.at[pl.ds(there, terms), rows]
            copies.append(
                pltpu.make_async_copy(from_ref, kept_ref.at[pl.ds(here, terms), rows], sems.at[piece, step])
            )
    return copies


def arrival(pieces, kept_ref, sems):
    def arrive(step):
        rows = pl.ds(pl.multiple_of(step * ROWS, ROWS), ROWS)
        for piece, (source, there, here, terms) in enumerate(pieces):
            from_ref = source.at[pl.ds(there, terms), rows]
            pltpu.make_async_copy(from_ref, kept_ref.at[pl.ds(here, terms), rows], sems.at[piece, step]).wait()

    return arrive


def local_kernel(first, *refs):
    if first:
        off_ref, far_ref, source_ref, iterate_ref, rounded_ref, inverse_ref = refs[:6]
        base_ref, stencil_ref, near_ref, partial_ref, sems = refs[6:]
        pieces = [(off_ref, 0, 0, 1), (far_ref, 1, 1, NEAR - 1)]
        for copy in loads(pieces, stencil_ref, sems):
            copy.start()
        arrive = arrival(pieces, stencil_ref, sems)
    else:
        stencil_ref, source_ref, iterate_ref, rounded_ref, inverse_ref, base_ref, near_ref, partial_ref = refs
        arrive = None
    count, components, sites = rounded_ref.shape
    lane = lax.broadcasted_iota(jnp.int32, (components, sites), 1) % LX

    @pl.loop(0, count, unroll=8)
    def _(r):
        value = rounded_ref[r].astype(F32)
        after = jnp.where(lane == LX - 1, pltpu.roll(value, LX - 1, 1), pltpu.roll(value, sites - 1, 1))
        before = jnp.where(lane == 0, pltpu.roll(value, sites - LX + 1, 1), pltpu.roll(value, 1, 1))
        near_ref[0, r] = after.astype(BF16)
        near_ref[1, r] = before.astype(BF16)
        near_ref[2, r] = pltpu.roll(value, sites - LX, 1).astype(BF16)
        near_ref[3, r] = pltpu.roll(value, LX, 1).astype(BF16)

    blocks = [lambda o, i, k=k: stencil_ref[k, o, sixteen(i), :] for k in range(NEAR)]
    vectors = [lambda r, i: rounded_ref[r, sixteen(i), :]]
    for k in range(NEAR - 1):
        vectors.append(lambda r, i, k=k: near_ref[k, r, sixteen(i), :])

    def finish(r, rows, sums):
        left = source_ref[r, rows, :].astype(F32) - sums
        kept = iterate_ref[r, rows, :] - rounded_ref[r, rows, :].astype(F32)
        base_ref[r, rows, :] = kept + left * inverse_ref[rows, :]

    multiply(blocks, vectors, partial_ref, finish, arrive)


def vmem(count):
    return [pl.BlockSpec(memory_space=pltpu.VMEM)] * count


def hbm(count):
    return [pl.BlockSpec(memory_space=pltpu.HBM)] * count


def local(stencil, source, iterate, rounded, inverse):
    count, components, sites = rounded.shape
    first = isinstance(stencil, tuple)
    kept = (NEAR, components, components, sites)
    scratch = [
        pltpu.VMEM((4, count, components, sites), BF16),
        pltpu.VMEM((2, count, ROWS * 8, LANES), F32),
    ]
    if first:
        scratch.append(pltpu.SemaphoreType.DMA((2, components // ROWS)))
    base = jax.ShapeDtypeStruct(rounded.shape, F32)
    blocks = stencil if first else (stencil,)
    return pl.pallas_call(
        functools.partial(local_kernel, first),
        in_specs=(hbm(2) if first else vmem(1)) + vmem(4),
        out_specs=vmem(2) if first else vmem(1)[0],
        out_shape=[base, pltpu.VMEM(kept, BF16)] if first else base,
        scratch_shapes=scratch,
        compiler_params=SMALL,
        cost_estimate=pl.CostEstimate(flops=10**9, bytes_accessed=12 * 2**20, transcendentals=0),
        name="local",
    )(*blocks, source, iterate, rounded, inverse)


def remote_kernel(first, last, *refs):
    if first:
        whole_ref, z0_ref, z1_ref, t0_ref, t1_ref, base_ref, inverse_ref = refs[:7]
        iterate_ref, rounded_ref, stencil_ref, partial_ref, sems = refs[7:]
        pieces = [(whole_ref, NEAR, 0, stencil_ref.shape[0])]
        for copy in loads(pieces, stencil_ref, sems):
            copy.start()
        arrive = arrival(pieces, stencil_ref, sems)
    else:
        stencil_ref, z0_ref, z1_ref, t0_ref, t1_ref, base_ref, inverse_ref = refs[:7]
        if last:
            rounded_ref, partial_ref = refs[7:]
        else:
            iterate_ref, rounded_ref, partial_ref = refs[7:]
        arrive = None

    z_odd = lax.axis_index("xy") % 2
    t_odd = lax.axis_index("zt") % 2
    blocks, vectors = [], []
    for k, ref in ((z_odd, z0_ref), (1 - z_odd, z1_ref), (2 + t_odd, t0_ref), (3 - t_odd, t1_ref)):
        blocks.append(lambda o, i, k=k: stencil_ref[k, o, sixteen(i), :])
        vectors.append(lambda r, i, ref=ref: ref[r, sixteen(i), :])

    def finish(r, rows, sums):
        iterate = base_ref[r, rows, :] - sums * inverse_ref[rows, :]
        if not last:
            iterate_ref[r, rows, :] = iterate
        rounded_ref[r, rows, :] = iterate.astype(BF16)

    multiply(blocks, vectors, partial_ref, finish, arrive)


def remote(stencil, halos, base, inverse, first, last):
    count, components, sites = base.shape
    types = [BF16] if last else [F32, BF16]
    shapes = [jax.ShapeDtypeStruct(base.shape, t) for t in types]
    scratch = [pltpu.VMEM((2, count, ROWS * 8, LANES), F32)]
    if first:
        shapes.append(pltpu.VMEM((stencil.shape[0] - NEAR, components, components, sites), BF16))
        scratch.append(pltpu.SemaphoreType.DMA((1, components // ROWS)))
    return pl.pallas_call(
        functools.partial(remote_kernel, first, last),
        in_specs=(hbm(1) if first else vmem(1)) + vmem(6),
        out_specs=vmem(len(shapes)),
        out_shape=shapes,
        scratch_shapes=scratch,
        compiler_params=SMALL,
        cost_estimate=pl.CostEstimate(flops=10**9, bytes_accessed=12 * 2**20, transcendentals=0),
        name="remote",
    )(stencil, *halos, base, inverse)


def pairs(plane, axis, first):
    count = lax.axis_size(axis)
    swaps = []
    for i in range(first, first + count, 2):
        a, b = i % count, (i + 1) % count
        swaps += [(a, b), (b, a)]
    return lax.ppermute(plane, axis, swaps)


def groups():
    columns = lax.axis_size("xy")
    return [list(range(i * columns, (i + 2) * columns)) for i in range(0, lax.axis_size("zt"), 2)]


def exchange(chunks):
    return lax.all_to_all(chunks, ("zt", "xy"), 0, 0, axis_index_groups=groups(), tiled=True)


def shards(restricted, stencil):
    columns = lax.axis_size("xy")
    planes = columns // 2
    components, count, sites = restricted.shape[2:]
    rows = components * count
    cells = sites // columns
    stencil = pltpu.with_memory_space_constraint(stencil[0, 0], pltpu.HBM)
    off, inverse = prepare(stencil)

    chunks = split(restricted.reshape(rows, sites), planes, cells)
    received = exchange(chunks.reshape(2 * columns, cells, rows))
    source, iterate, rounded = start(received.reshape(2, sites, rows), inverse)
    for sweep in range(SWEEPS - 1):
        last = sweep == SWEEPS - 2
        halos = [
            pairs(rounded, "xy", 0),
            pairs(rounded, "xy", 1),
            pairs(rounded, "zt", 0),
            pairs(rounded, "zt", 1),
        ]
        if sweep == 0:
            base, near = local((off[None], stencil), source, iterate, rounded, inverse)
            iterate, rounded, far = remote(stencil, halos, base, inverse, True, False)
        elif not last:
            base = local(near, source, iterate, rounded, inverse)
            iterate, rounded = remote(far, halos, base, inverse, False, False)
        else:
            base = local(near, source, iterate, rounded, inverse)
            (rounded,) = remote(far, halos, base, inverse, False, True)

    chunks = leave(rounded, columns)
    received = exchange(chunks.reshape(2 * columns, cells, rows))
    result = join(received.reshape(2, 2, planes * cells, rows))
    return result.reshape(1, 1, components, count, sites)


def solution(mesh):
    placed = (P("zt", "xy", None, None, None), P("zt", "xy", None, None, None, None))
    return jax.shard_map(
        shards,
        mesh=mesh,
        in_specs=placed,
        out_specs=P("zt", "xy", None, None, None),
        check_vma=False,
    )
```

```python
import functools

import jax
import jax.numpy as jnp
from jax import lax
from jax.experimental import pallas as pl
from jax.experimental.pallas import tpu as pltpu
from jax.sharding import PartitionSpec as P

LX = 16
LY = 16
SWEEPS = 4
ROWS = 16
NEAR = 5
PAIR = 1
GROUP = 8
TERMS = 2
LANES = 128
F32 = jnp.float32
BF16 = jnp.bfloat16
SMALL = pltpu.CompilerParams(vmem_limit_bytes=8 * 2**20)


def total(terms):
    while len(terms) > 1:
        terms = [sum(terms[i : i + 2][1:], terms[i]) for i in range(0, len(terms), 2)]
    return terms[0]


def multiply(blocks, vectors, partial_ref, finish, arrive=None):
    _, count, _, _ = partial_ref.shape
    components = 64

    @pl.loop(0, components // ROWS)
    def _(step):
        start = pl.multiple_of(step * ROWS, ROWS)
        if arrive is not None:
            arrive(step)

        @pl.loop(0, ROWS // PAIR, unroll=4)
        def _(pair):
            row = start + pair * PAIR
            for first in range(0, count, GROUP):
                sums = {}
                for k in range(0, len(blocks), TERMS):
                    some = list(zip(blocks, vectors))[k : k + TERMS]
                    rows = [
                        [block(row + o, i) for block, _ in some for i in range(components // 16)] for o in range(PAIR)
                    ]
                    for r in range(first, first + GROUP):
                        column = [vector(r, i) for _, vector in some for i in range(components // 16)]
                        for o in range(PAIR):
                            term = total([a * v for a, v in zip(rows[o], column)])
                            term = (term[:8] + term[8:]).astype(F32)
                            sums[o, r] = sums[o, r] + term if (o, r) in sums else term
                for (o, r), value in sums.items():
                    place = pl.ds(pl.multiple_of((pair * PAIR + o) * 8, 8), 8)
                    partial_ref[0, r, place, :] = value[:, :LANES]
                    partial_ref[1, r, place, :] = value[:, LANES:]

        for r in range(count):
            sums = [
                [
                    total([partial_ref[half, r, pl.ds(eight * 64 + j, 8, stride=8), :] for j in range(8)])
                    for half in range(2)
                ]
                for eight in range(ROWS // 8)
            ]
            sums = jnp.concatenate([jnp.concatenate(halves, axis=1) for halves in sums], axis=0)
            finish(r, pl.ds(start, ROWS), sums)


def prepare_kernel(block_ref, off_ref, inverse_ref):
    components, _, sites = off_ref.shape
    off_ref[...] = block_ref[0]

    @pl.loop(0, components // 16)
    def _(group):
        first = pl.multiple_of(group * 16, 16)
        here = lax.broadcasted_iota(jnp.int32, (16, sites), 0)
        diagonal = jnp.zeros((16, sites), F32)
        for o in range(16):
            block = block_ref[0, first + o, pl.ds(first, 16), :].astype(F32)
            diagonal = jnp.where(here == o, block, diagonal)
            off_ref[first + o, pl.ds(first, 16), :] = jnp.where(here == o, 0.0, block).astype(BF16)
        inverse_ref[pl.ds(first, 16), :] = 1.0 / diagonal


def prepare(stencil):
    _, components, _, sites = stencil.shape
    shape = (components, components, sites)
    return pl.pallas_call(
        prepare_kernel,
        grid=(1,),
        in_specs=[pl.BlockSpec((1, *shape), lambda g: (0, 0, 0, 0))],
        out_specs=[pl.BlockSpec(shape, lambda g: (0, 0, 0)), pl.BlockSpec((components, sites), lambda g: (0, 0))],
        out_shape=[jax.ShapeDtypeStruct(shape, BF16), jax.ShapeDtypeStruct((components, sites), F32)],
        compiler_params=pltpu.CompilerParams(vmem_limit_bytes=16 * 2**20),
        cost_estimate=pl.CostEstimate(flops=10**7, bytes_accessed=4 * 2**20, transcendentals=0),
        name="prepare",
    )(stencil)


def one_hot(index, size):
    column = lax.broadcasted_iota(jnp.int32, (size, size), 1)
    return jnp.where(column == index, 1.0, 0.0).astype(BF16)


def fine_order(sites):
    place = lax.broadcasted_iota(jnp.int32, (sites, sites), 0)
    u, w, g, h = place // 64, place // 16 % 4, place // 4 % 4, place % 4
    return u * 64 + g * 16 + w * 4 + h


def split_kernel(fine_ref, out_ref):
    rows, sites = fine_ref.shape
    _, _, planes, cells, _ = out_ref.shape
    unit = one_hot(lax.broadcasted_iota(jnp.int32, (sites, sites), 0), sites)
    turned = lax.dot_general(unit, fine_ref[...], (((1,), (1,)), ((), ())), preferred_element_type=F32)
    turned = turned.astype(BF16).reshape(2, planes, cells, rows)
    for half in range(2):
        out_ref[:, half] = turned


def split(fine, planes, cells):
    rows, _ = fine.shape
    return pl.pallas_call(
        split_kernel,
        out_shape=jax.ShapeDtypeStruct((2, 2, planes, cells, rows), BF16),
        compiler_params=SMALL,
        name="split",
    )(fine)


def start_kernel(received_ref, inverse_ref, source_ref, iterate_ref, rounded_ref, turned_ref):
    count, components, sites = rounded_ref.shape
    half = lax.axis_index("xy") // (lax.axis_size("xy") // 2)
    order = one_hot(fine_order(sites), sites)
    turned = lax.dot_general(
        received_ref[half], order, (((0,), (0,)), ((), ())), preferred_element_type=F32
    )
    for i in range(sites // LANES):
        turned_ref[i] = turned[:, i * LANES : (i + 1) * LANES]
    inverse = inverse_ref[...]
    for r in range(count):
        source = jnp.concatenate(
            [turned_ref[i, pl.ds(r, components, stride=count), :] for i in range(sites // LANES)], axis=1
        )
        iterate = source * inverse
        source_ref[r] = source.astype(BF16)
        iterate_ref[r] = iterate
        rounded_ref[r] = iterate.astype(BF16)


def start(received, inverse):
    _, sites, rows = received.shape
    components = inverse.shape[0]
    shape = (rows // components, components, sites)
    return pl.pallas_call(
        start_kernel,
        out_shape=[jax.ShapeDtypeStruct(shape, t) for t in (BF16, F32, BF16)],
        scratch_shapes=[pltpu.VMEM((sites // LANES, rows, LANES), F32)],
        compiler_params=SMALL,
        name="start",
    )(received, inverse)


def leave_kernel(rounded_ref, out_ref, mixed_ref):
    count, components, sites = rounded_ref.shape
    _, columns, cells, rows = out_ref.shape
    for r in range(count):
        value = rounded_ref[r].astype(F32)
        for i in range(sites // LANES):
            mixed_ref[i, pl.ds(r, components, stride=count), :] = value[:, i * LANES : (i + 1) * LANES]
    mixed = jnp.concatenate([mixed_ref[i].astype(BF16) for i in range(sites // LANES)], axis=1)
    order = one_hot(fine_order(sites), sites)
    turned = lax.dot_general(order, mixed, (((1,), (1,)), ((), ())), preferred_element_type=F32)
    turned = turned.astype(BF16).reshape(columns, cells, rows)
    for half in range(2):
        out_ref[half] = turned


def leave(rounded, columns):
    count, components, sites = rounded.shape
    rows = count * components
    return pl.pallas_call(
        leave_kernel,
        out_shape=jax.ShapeDtypeStruct((2, columns, sites // columns, rows), BF16),
        scratch_shapes=[pltpu.VMEM((sites // LANES, rows, LANES), F32)],
        compiler_params=SMALL,
        name="leave",
    )(rounded)


def join_kernel(received_ref, out_ref):
    places = received_ref.shape[2]
    half = lax.axis_index("zt") % 2
    unit = one_hot(lax.broadcasted_iota(jnp.int32, (places, places), 0), places)
    for e in range(2):
        out_ref[:, places * e : places * (e + 1)] = lax.dot_general(
            received_ref[e, half], unit, (((0,), (0,)), ((), ())), preferred_element_type=F32
        )


def join(received):
    _, _, places, rows = received.shape
    return pl.pallas_call(
        join_kernel,
        out_shape=jax.ShapeDtypeStruct((rows, 2 * places), F32),
        compiler_params=SMALL,
        name="join",
    )(received)


def sixteen(i):
    return slice(16 * i, 16 * i + 16)


def loads(pieces, kept_ref, sems):
    copies = []
    for step in range(kept_ref.shape[1] // ROWS):
        rows = pl.ds(step * ROWS, ROWS)
        for piece, (source, there, here, terms) in enumerate(pieces):
            from_ref = source.at[pl.ds(there, terms), rows]
            copies.append(
                pltpu.make_async_copy(from_ref, kept_ref.at[pl.ds(here, terms), rows], sems.at[piece, step])
            )
    return copies


def arrival(pieces, kept_ref, sems):
    def arrive(step):
        rows = pl.ds(pl.multiple_of(step * ROWS, ROWS), ROWS)
        for piece, (source, there, here, terms) in enumerate(pieces):
            from_ref = source.at[pl.ds(there, terms), rows]
            pltpu.make_async_copy(from_ref, kept_ref.at[pl.ds(here, terms), rows], sems.at[piece, step]).wait()

    return arrive


def local_kernel(first, *refs):
    if first:
        off_ref, far_ref, source_ref, iterate_ref, rounded_ref, inverse_ref = refs[:6]
        base_ref, stencil_ref, far_kept_ref, near_ref, partial_ref, sems, far_sems = refs[6:]
        pieces = [(off_ref, 0, 0, 1), (far_ref, 1, 1, NEAR - 1)]
        far_copies = loads([(far_ref, NEAR, 0, far_kept_ref.shape[0])], far_kept_ref, far_sems)
        for copy in loads(pieces, stencil_ref, sems) + far_copies:
            copy.start()
        arrive = arrival(pieces, stencil_ref, sems)
    else:
        stencil_ref, source_ref, iterate_ref, rounded_ref, inverse_ref, base_ref, near_ref, partial_ref = refs
        arrive = None
    count, components, sites = rounded_ref.shape
    lane = lax.broadcasted_iota(jnp.int32, (components, sites), 1) % LX

    @pl.loop(0, count, unroll=8)
    def _(r):
        value = rounded_ref[r].astype(F32)
        after = jnp.where(lane == LX - 1, pltpu.roll(value, LX - 1, 1), pltpu.roll(value, sites - 1, 1))
        before = jnp.where(lane == 0, pltpu.roll(value, sites - LX + 1, 1), pltpu.roll(value, 1, 1))
        near_ref[0, r] = after.astype(BF16)
        near_ref[1, r] = before.astype(BF16)
        near_ref[2, r] = pltpu.roll(value, sites - LX, 1).astype(BF16)
        near_ref[3, r] = pltpu.roll(value, LX, 1).astype(BF16)

    blocks = [lambda o, i, k=k: stencil_ref[k, o, sixteen(i), :] for k in range(NEAR)]
    vectors = [lambda r, i: rounded_ref[r, sixteen(i), :]]
    for k in range(NEAR - 1):
        vectors.append(lambda r, i, k=k: near_ref[k, r, sixteen(i), :])

    def finish(r, rows, sums):
        left = source_ref[r, rows, :].astype(F32) - sums
        kept = iterate_ref[r, rows, :] - rounded_ref[r, rows, :].astype(F32)
        base_ref[r, rows, :] = kept + left * inverse_ref[rows, :]

    multiply(blocks, vectors, partial_ref, finish, arrive)
    if first:
        for copy in far_copies:
            copy.wait()


def vmem(count):
    return [pl.BlockSpec(memory_space=pltpu.VMEM)] * count


def hbm(count):
    return [pl.BlockSpec(memory_space=pltpu.HBM)] * count


def local(stencil, source, iterate, rounded, inverse):
    count, components, sites = rounded.shape
    first = isinstance(stencil, tuple)
    block = (components, components, sites)
    scratch = [
        pltpu.VMEM((4, count, components, sites), BF16),
        pltpu.VMEM((2, count, ROWS * 8, LANES), F32),
    ]
    if first:
        scratch.append(pltpu.SemaphoreType.DMA((2, components // ROWS)))
        scratch.append(pltpu.SemaphoreType.DMA((1, components // ROWS)))
    base = jax.ShapeDtypeStruct(rounded.shape, F32)
    blocks = stencil if first else (stencil,)
    return pl.pallas_call(
        functools.partial(local_kernel, first),
        in_specs=(hbm(2) if first else vmem(1)) + vmem(4),
        out_specs=vmem(3) if first else vmem(1)[0],
        out_shape=(
            [base, pltpu.VMEM((NEAR, *block), BF16), pltpu.VMEM((stencil[1].shape[0] - NEAR, *block), BF16)]
            if first
            else base
        ),
        scratch_shapes=scratch,
        compiler_params=SMALL,
        cost_estimate=pl.CostEstimate(flops=10**9, bytes_accessed=12 * 2**20, transcendentals=0),
        name="local",
    )(*blocks, source, iterate, rounded, inverse)


def remote_kernel(last, *refs):
    stencil_ref, t0_ref, t1_ref, z0_ref, z1_ref, base_ref, inverse_ref = refs[:7]
    if last:
        rounded_ref, partial_ref = refs[7:]
    else:
        iterate_ref, rounded_ref, partial_ref = refs[7:]

    z_odd = lax.axis_index("xy") % 2
    t_odd = lax.axis_index("zt") % 2
    blocks, vectors = [], []
    for k, ref in ((z_odd, z0_ref), (1 - z_odd, z1_ref), (2 + t_odd, t0_ref), (3 - t_odd, t1_ref)):
        blocks.append(lambda o, i, k=k: stencil_ref[k, o, sixteen(i), :])
        vectors.append(lambda r, i, ref=ref: ref[r, sixteen(i), :])

    def finish(r, rows, sums):
        iterate = base_ref[r, rows, :] - sums * inverse_ref[rows, :]
        if not last:
            iterate_ref[r, rows, :] = iterate
        rounded_ref[r, rows, :] = iterate.astype(BF16)

    multiply(blocks, vectors, partial_ref, finish)


def remote(stencil, halos, base, inverse, last):
    count = base.shape[0]
    types = [BF16] if last else [F32, BF16]
    return pl.pallas_call(
        functools.partial(remote_kernel, last),
        in_specs=vmem(7),
        out_specs=vmem(len(types)),
        out_shape=[jax.ShapeDtypeStruct(base.shape, t) for t in types],
        scratch_shapes=[pltpu.VMEM((2, count, ROWS * 8, LANES), F32)],
        compiler_params=SMALL,
        cost_estimate=pl.CostEstimate(flops=10**9, bytes_accessed=12 * 2**20, transcendentals=0),
        name="remote",
    )(stencil, *halos, base, inverse)


def pairs(plane, axis, first):
    count = lax.axis_size(axis)
    swaps = []
    for i in range(first, first + count, 2):
        a, b = i % count, (i + 1) % count
        swaps += [(a, b), (b, a)]
    return lax.ppermute(plane, axis, swaps)


def groups():
    columns = lax.axis_size("xy")
    return [list(range(i * columns, (i + 2) * columns)) for i in range(0, lax.axis_size("zt"), 2)]


def exchange(chunks):
    return lax.all_to_all(chunks, ("zt", "xy"), 0, 0, axis_index_groups=groups(), tiled=True)


def shards(restricted, stencil):
    columns = lax.axis_size("xy")
    planes = columns // 2
    components, count, sites = restricted.shape[2:]
    rows = components * count
    cells = sites // columns
    stencil = pltpu.with_memory_space_constraint(stencil[0, 0], pltpu.HBM)
    off, inverse = prepare(stencil)

    chunks = split(restricted.reshape(rows, sites), planes, cells)
    received = exchange(chunks.reshape(2 * columns, cells, rows))
    source, iterate, rounded = start(received.reshape(2, sites, rows), inverse)
    for sweep in range(SWEEPS - 1):
        last = sweep == SWEEPS - 2
        halos = [
            pairs(rounded, "zt", 0),
            pairs(rounded, "zt", 1),
            pairs(rounded, "xy", 0),
            pairs(rounded, "xy", 1),
        ]
        if sweep == 0:
            base, near, far = local((off[None], stencil), source, iterate, rounded, inverse)
        else:
            base = local(near, source, iterate, rounded, inverse)
        *iterate, rounded = remote(far, halos, base, inverse, last)
        iterate = None if last else iterate[0]

    chunks = leave(rounded, columns)
    received = exchange(chunks.reshape(2 * columns, cells, rows))
    result = join(received.reshape(2, 2, planes * cells, rows))
    return result.reshape(1, 1, components, count, sites)


def solution(mesh):
    placed = (P("zt", "xy", None, None, None), P("zt", "xy", None, None, None, None))
    return jax.shard_map(
        shards,
        mesh=mesh,
        in_specs=placed,
        out_specs=P("zt", "xy", None, None, None),
        check_vma=False,
    )
```

```python
import functools

import jax
import jax.numpy as jnp
from jax import lax
from jax.experimental import pallas as pl
from jax.experimental.pallas import tpu as pltpu
from jax.sharding import PartitionSpec as P

LX = 16
LY = 16
SWEEPS = 4
ROWS = 16
NEAR = 5
PAIR = 1
GROUP = 8
TERMS = 2
LANES = 128
F32 = jnp.float32
BF16 = jnp.bfloat16
SMALL = pltpu.CompilerParams(vmem_limit_bytes=8 * 2**20)


def total(terms):
    while len(terms) > 1:
        terms = [sum(terms[i : i + 2][1:], terms[i]) for i in range(0, len(terms), 2)]
    return terms[0]


def multiply(blocks, vectors, partial_ref, finish, arrive=None):
    _, count, _, _ = partial_ref.shape
    components = 64

    @pl.loop(0, components // ROWS)
    def _(step):
        start = pl.multiple_of(step * ROWS, ROWS)
        if arrive is not None:
            arrive(step)

        @pl.loop(0, ROWS // PAIR, unroll=8)
        def _(pair):
            row = start + pair * PAIR
            for first in range(0, count, GROUP):
                sums = {}
                for k in range(0, len(blocks), TERMS):
                    some = list(zip(blocks, vectors))[k : k + TERMS]
                    rows = [
                        [block(row + o, i) for block, _ in some for i in range(components // 16)] for o in range(PAIR)
                    ]
                    for r in range(first, first + GROUP):
                        column = [vector(r, i) for _, vector in some for i in range(components // 16)]
                        for o in range(PAIR):
                            term = total([a * v for a, v in zip(rows[o], column)])
                            term = (term[:8] + term[8:]).astype(F32)
                            sums[o, r] = sums[o, r] + term if (o, r) in sums else term
                for (o, r), value in sums.items():
                    place = pl.ds(pl.multiple_of((pair * PAIR + o) * 8, 8), 8)
                    partial_ref[0, r, place, :] = value[:, :LANES]
                    partial_ref[1, r, place, :] = value[:, LANES:]

        for r in range(count):
            sums = [
                [
                    total([partial_ref[half, r, pl.ds(eight * 64 + j, 8, stride=8), :] for j in range(8)])
                    for half in range(2)
                ]
                for eight in range(ROWS // 8)
            ]
            sums = jnp.concatenate([jnp.concatenate(halves, axis=1) for halves in sums], axis=0)
            finish(r, pl.ds(start, ROWS), sums)


def prepare_kernel(block_ref, off_ref, inverse_ref):
    components, _, sites = off_ref.shape
    off_ref[...] = block_ref[0]

    @pl.loop(0, components // 16)
    def _(group):
        first = pl.multiple_of(group * 16, 16)
        here = lax.broadcasted_iota(jnp.int32, (16, sites), 0)
        diagonal = jnp.zeros((16, sites), F32)
        for o in range(16):
            block = block_ref[0, first + o, pl.ds(first, 16), :].astype(F32)
            diagonal = jnp.where(here == o, block, diagonal)
            off_ref[first + o, pl.ds(first, 16), :] = jnp.where(here == o, 0.0, block).astype(BF16)
        inverse_ref[pl.ds(first, 16), :] = 1.0 / diagonal


def prepare(stencil):
    _, components, _, sites = stencil.shape
    shape = (components, components, sites)
    return pl.pallas_call(
        prepare_kernel,
        grid=(1,),
        in_specs=[pl.BlockSpec((1, *shape), lambda g: (0, 0, 0, 0))],
        out_specs=[pl.BlockSpec(shape, lambda g: (0, 0, 0)), pl.BlockSpec((components, sites), lambda g: (0, 0))],
        out_shape=[jax.ShapeDtypeStruct(shape, BF16), jax.ShapeDtypeStruct((components, sites), F32)],
        compiler_params=pltpu.CompilerParams(vmem_limit_bytes=16 * 2**20),
        cost_estimate=pl.CostEstimate(flops=10**7, bytes_accessed=4 * 2**20, transcendentals=0),
        name="prepare",
    )(stencil)


def one_hot(index, size):
    column = lax.broadcasted_iota(jnp.int32, (size, size), 1)
    return jnp.where(column == index, 1.0, 0.0).astype(BF16)


def fine_order(sites):
    place = lax.broadcasted_iota(jnp.int32, (sites, sites), 0)
    u, w, g, h = place // 64, place // 16 % 4, place // 4 % 4, place % 4
    return u * 64 + g * 16 + w * 4 + h


def split_kernel(fine_ref, out_ref):
    rows, sites = fine_ref.shape
    _, _, planes, cells, _ = out_ref.shape
    unit = one_hot(lax.broadcasted_iota(jnp.int32, (sites, sites), 0), sites)
    turned = lax.dot_general(unit, fine_ref[...], (((1,), (1,)), ((), ())), preferred_element_type=F32)
    turned = turned.astype(BF16).reshape(2, planes, cells, rows)
    for half in range(2):
        out_ref[:, half] = turned


def split(fine, planes, cells):
    rows, _ = fine.shape
    return pl.pallas_call(
        split_kernel,
        out_shape=jax.ShapeDtypeStruct((2, 2, planes, cells, rows), BF16),
        compiler_params=SMALL,
        name="split",
    )(fine)


def start_kernel(received_ref, inverse_ref, source_ref, iterate_ref, rounded_ref, turned_ref):
    count, components, sites = rounded_ref.shape
    half = lax.axis_index("xy") // (lax.axis_size("xy") // 2)
    order = one_hot(fine_order(sites), sites)
    turned = lax.dot_general(
        received_ref[half], order, (((0,), (0,)), ((), ())), preferred_element_type=F32
    )
    for i in range(sites // LANES):
        turned_ref[i] = turned[:, i * LANES : (i + 1) * LANES]
    inverse = inverse_ref[...]
    for r in range(count):
        source = jnp.concatenate(
            [turned_ref[i, pl.ds(r, components, stride=count), :] for i in range(sites // LANES)], axis=1
        )
        iterate = source * inverse
        source_ref[r] = source.astype(BF16)
        iterate_ref[r] = iterate
        rounded_ref[r] = iterate.astype(BF16)


def start(received, inverse):
    _, sites, rows = received.shape
    components = inverse.shape[0]
    shape = (rows // components, components, sites)
    return pl.pallas_call(
        start_kernel,
        out_shape=[jax.ShapeDtypeStruct(shape, t) for t in (BF16, F32, BF16)],
        scratch_shapes=[pltpu.VMEM((sites // LANES, rows, LANES), F32)],
        compiler_params=SMALL,
        name="start",
    )(received, inverse)


def leave_kernel(rounded_ref, out_ref, mixed_ref):
    count, components, sites = rounded_ref.shape
    _, columns, cells, rows = out_ref.shape
    for r in range(count):
        value = rounded_ref[r].astype(F32)
        for i in range(sites // LANES):
            mixed_ref[i, pl.ds(r, components, stride=count), :] = value[:, i * LANES : (i + 1) * LANES]
    mixed = jnp.concatenate([mixed_ref[i].astype(BF16) for i in range(sites // LANES)], axis=1)
    order = one_hot(fine_order(sites), sites)
    turned = lax.dot_general(order, mixed, (((1,), (1,)), ((), ())), preferred_element_type=F32)
    turned = turned.astype(BF16).reshape(columns, cells, rows)
    for half in range(2):
        out_ref[half] = turned


def leave(rounded, columns):
    count, components, sites = rounded.shape
    rows = count * components
    return pl.pallas_call(
        leave_kernel,
        out_shape=jax.ShapeDtypeStruct((2, columns, sites // columns, rows), BF16),
        scratch_shapes=[pltpu.VMEM((sites // LANES, rows, LANES), F32)],
        compiler_params=SMALL,
        name="leave",
    )(rounded)


def join_kernel(received_ref, out_ref):
    places = received_ref.shape[2]
    half = lax.axis_index("zt") % 2
    unit = one_hot(lax.broadcasted_iota(jnp.int32, (places, places), 0), places)
    for e in range(2):
        out_ref[:, places * e : places * (e + 1)] = lax.dot_general(
            received_ref[e, half], unit, (((0,), (0,)), ((), ())), preferred_element_type=F32
        )


def join(received):
    _, _, places, rows = received.shape
    return pl.pallas_call(
        join_kernel,
        out_shape=jax.ShapeDtypeStruct((rows, 2 * places), F32),
        compiler_params=SMALL,
        name="join",
    )(received)


def sixteen(i):
    return slice(16 * i, 16 * i + 16)


def loads(pieces, kept_ref, sems):
    copies = []
    for step in range(kept_ref.shape[1] // ROWS):
        rows = pl.ds(step * ROWS, ROWS)
        for piece, (source, there, here, terms) in enumerate(pieces):
            from_ref = source.at[pl.ds(there, terms), rows]
            copies.append(
                pltpu.make_async_copy(from_ref, kept_ref.at[pl.ds(here, terms), rows], sems.at[piece, step])
            )
    return copies


def arrival(pieces, kept_ref, sems):
    def arrive(step):
        rows = pl.ds(pl.multiple_of(step * ROWS, ROWS), ROWS)
        for piece, (source, there, here, terms) in enumerate(pieces):
            from_ref = source.at[pl.ds(there, terms), rows]
            pltpu.make_async_copy(from_ref, kept_ref.at[pl.ds(here, terms), rows], sems.at[piece, step]).wait()

    return arrive


def local_kernel(first, *refs):
    if first:
        off_ref, far_ref, source_ref, iterate_ref, rounded_ref, inverse_ref = refs[:6]
        base_ref, stencil_ref, far_kept_ref, near_ref, partial_ref, sems, far_sems = refs[6:]
        pieces = [(off_ref, 0, 0, 1), (far_ref, 1, 1, NEAR - 1)]
        far_copies = loads([(far_ref, NEAR, 0, far_kept_ref.shape[0])], far_kept_ref, far_sems)
        for copy in loads(pieces, stencil_ref, sems) + far_copies:
            copy.start()
        arrive = arrival(pieces, stencil_ref, sems)
    else:
        stencil_ref, source_ref, iterate_ref, rounded_ref, inverse_ref, base_ref, near_ref, partial_ref = refs
        arrive = None
    count, components, sites = rounded_ref.shape
    lane = lax.broadcasted_iota(jnp.int32, (components, sites), 1) % LX

    @pl.loop(0, count, unroll=8)
    def _(r):
        value = rounded_ref[r].astype(F32)
        after = jnp.where(lane == LX - 1, pltpu.roll(value, LX - 1, 1), pltpu.roll(value, sites - 1, 1))
        before = jnp.where(lane == 0, pltpu.roll(value, sites - LX + 1, 1), pltpu.roll(value, 1, 1))
        near_ref[0, r] = after.astype(BF16)
        near_ref[1, r] = before.astype(BF16)
        near_ref[2, r] = pltpu.roll(value, sites - LX, 1).astype(BF16)
        near_ref[3, r] = pltpu.roll(value, LX, 1).astype(BF16)

    blocks = [lambda o, i, k=k: stencil_ref[k, o, sixteen(i), :] for k in range(NEAR)]
    vectors = [lambda r, i: rounded_ref[r, sixteen(i), :]]
    for k in range(NEAR - 1):
        vectors.append(lambda r, i, k=k: near_ref[k, r, sixteen(i), :])

    def finish(r, rows, sums):
        left = source_ref[r, rows, :].astype(F32) - sums
        kept = iterate_ref[r, rows, :] - rounded_ref[r, rows, :].astype(F32)
        base_ref[r, rows, :] = kept + left * inverse_ref[rows, :]

    multiply(blocks, vectors, partial_ref, finish, arrive)
    if first:
        for copy in far_copies:
            copy.wait()


def vmem(count):
    return [pl.BlockSpec(memory_space=pltpu.VMEM)] * count


def hbm(count):
    return [pl.BlockSpec(memory_space=pltpu.HBM)] * count


def local(stencil, source, iterate, rounded, inverse):
    count, components, sites = rounded.shape
    first = isinstance(stencil, tuple)
    block = (components, components, sites)
    scratch = [
        pltpu.VMEM((4, count, components, sites), BF16),
        pltpu.VMEM((2, count, ROWS * 8, LANES), F32),
    ]
    if first:
        scratch.append(pltpu.SemaphoreType.DMA((2, components // ROWS)))
        scratch.append(pltpu.SemaphoreType.DMA((1, components // ROWS)))
    base = jax.ShapeDtypeStruct(rounded.shape, F32)
    blocks = stencil if first else (stencil,)
    return pl.pallas_call(
        functools.partial(local_kernel, first),
        in_specs=(hbm(2) if first else vmem(1)) + vmem(4),
        out_specs=vmem(3) if first else vmem(1)[0],
        out_shape=(
            [base, pltpu.VMEM((NEAR, *block), BF16), pltpu.VMEM((stencil[1].shape[0] - NEAR, *block), BF16)]
            if first
            else base
        ),
        scratch_shapes=scratch,
        compiler_params=SMALL,
        cost_estimate=pl.CostEstimate(flops=10**9, bytes_accessed=12 * 2**20, transcendentals=0),
        name="local",
    )(*blocks, source, iterate, rounded, inverse)


def remote_kernel(last, *refs):
    stencil_ref, t0_ref, t1_ref, z0_ref, z1_ref, base_ref, inverse_ref = refs[:7]
    if last:
        rounded_ref, partial_ref = refs[7:]
    else:
        iterate_ref, rounded_ref, partial_ref = refs[7:]

    z_odd = lax.axis_index("xy") % 2
    t_odd = lax.axis_index("zt") % 2
    blocks, vectors = [], []
    for k, ref in ((z_odd, z0_ref), (1 - z_odd, z1_ref), (2 + t_odd, t0_ref), (3 - t_odd, t1_ref)):
        blocks.append(lambda o, i, k=k: stencil_ref[k, o, sixteen(i), :])
        vectors.append(lambda r, i, ref=ref: ref[r, sixteen(i), :])

    def finish(r, rows, sums):
        iterate = base_ref[r, rows, :] - sums * inverse_ref[rows, :]
        if not last:
            iterate_ref[r, rows, :] = iterate
        rounded_ref[r, rows, :] = iterate.astype(BF16)

    multiply(blocks, vectors, partial_ref, finish)


def remote(stencil, halos, base, inverse, last):
    count = base.shape[0]
    types = [BF16] if last else [F32, BF16]
    return pl.pallas_call(
        functools.partial(remote_kernel, last),
        in_specs=vmem(7),
        out_specs=vmem(len(types)),
        out_shape=[jax.ShapeDtypeStruct(base.shape, t) for t in types],
        scratch_shapes=[pltpu.VMEM((2, count, ROWS * 8, LANES), F32)],
        compiler_params=SMALL,
        cost_estimate=pl.CostEstimate(flops=10**9, bytes_accessed=12 * 2**20, transcendentals=0),
        name="remote",
    )(stencil, *halos, base, inverse)


def pairs(plane, axis, first):
    count = lax.axis_size(axis)
    swaps = []
    for i in range(first, first + count, 2):
        a, b = i % count, (i + 1) % count
        swaps += [(a, b), (b, a)]
    return lax.ppermute(plane, axis, swaps)


def groups():
    columns = lax.axis_size("xy")
    return [list(range(i * columns, (i + 2) * columns)) for i in range(0, lax.axis_size("zt"), 2)]


def exchange(chunks):
    return lax.all_to_all(chunks, ("zt", "xy"), 0, 0, axis_index_groups=groups(), tiled=True)


def shards(restricted, stencil):
    columns = lax.axis_size("xy")
    planes = columns // 2
    components, count, sites = restricted.shape[2:]
    rows = components * count
    cells = sites // columns
    stencil = pltpu.with_memory_space_constraint(stencil[0, 0], pltpu.HBM)
    off, inverse = prepare(stencil)

    chunks = split(restricted.reshape(rows, sites), planes, cells)
    received = exchange(chunks.reshape(2 * columns, cells, rows))
    source, iterate, rounded = start(received.reshape(2, sites, rows), inverse)
    for sweep in range(SWEEPS - 1):
        last = sweep == SWEEPS - 2
        halos = [
            pairs(rounded, "zt", 0),
            pairs(rounded, "zt", 1),
            pairs(rounded, "xy", 0),
            pairs(rounded, "xy", 1),
        ]
        if sweep == 0:
            base, near, far = local((off[None], stencil), source, iterate, rounded, inverse)
        else:
            base = local(near, source, iterate, rounded, inverse)
        *iterate, rounded = remote(far, halos, base, inverse, last)
        iterate = None if last else iterate[0]

    chunks = leave(rounded, columns)
    received = exchange(chunks.reshape(2 * columns, cells, rows))
    result = join(received.reshape(2, 2, planes * cells, rows))
    return result.reshape(1, 1, components, count, sites)


def solution(mesh):
    placed = (P("zt", "xy", None, None, None), P("zt", "xy", None, None, None, None))
    return jax.shard_map(
        shards,
        mesh=mesh,
        in_specs=placed,
        out_specs=P("zt", "xy", None, None, None),
        check_vma=False,
    )
```
